128 devices in a mesh: dom: 128 (over y, z, x, core).
Axes of the slice: x: 4, y: 4, z: 4, core: 2. Of those that a mesh axis runs over, the one named last changes fastest.
Arguments:
- elem_state: bfloat16 [4096, 5, 216], P('dom'), may hold values from -6 to 6
- mass_inverse: bfloat16 [4096, 216, 216], P('dom'), as said below
- jacobian: bfloat16 [4096, 216, 216], P('dom'), may hold values from -0.4375 to 0.4375
- elem_order: int32 [4096], P('dom'), may hold values from 2 to 5
- new_owner: int32 [4096], P('dom'), may hold values from 0 to 127, as said below
- neighbors: int32 [4096, 6], P('dom'), may hold values from -1 to 4095, as said below
- penalty: bfloat16 [4096, 6], P('dom'), may hold values from 0.049804688 to 0.5
- closure_in: bfloat16 [64, 5], replicated, may hold values from -2.5 to 2.5
- closure_out: bfloat16 [5, 64], replicated, may hold values from -0.75 to 0.75
Outputs:
- migrated: float32 [6144, 5, 216], P('dom')
- migrated_mass: bfloat16 [6144, 216, 216], P('dom')
- migrated_jacobian: bfloat16 [6144, 216, 216], P('dom')
The draws below stay inside these ranges and needn't reach their ends.
Inputs may be any that keep to these rules, and one draw needn't show every extreme that they name: new_owner never falls along the elements; each element's new owner is the device that holds it before the repartition (32 elements a device, in order) or a device beside that one; at most 8 elements pass from one device to each neighbour, and each device owns between 16 and 48 elements afterwards; 8 and 48 are reached. `neighbors`: each entry is -1 or an element within 16 places of its own element along the curve; the distance 16 is reached. `mass_inverse`: each tile has a diagonal of order one and small off-diagonal entries.
All inputs are finite; a program needn't handle non-finite values.
Results may differ from the reference program's by a relative error of at most 0.01.
Values may be sent and summed in bfloat16 or wider, within the bound.
A program may use at most 128 MiB of HBM per device.

```python
import math
import jax
import jax.numpy as jnp
from jax import lax

NODE = 216
VARS = 5
HID = 64
FACES = 6
SWEEPS = 2
E_DEV = 32
MOVE = 8
CAP = 48
REACH = 16
ELEMS = 4096
N_DOM = 128


def draw_mass_inverse(key, part):
    first_key, second_key = jax.random.split(jax.random.fold_in(key, 11))
    node_ids = jnp.arange(NODE)
    diagonal = jax.random.uniform(first_key, (ELEMS, NODE), jnp.float32, 0.6, 1.6)
    spread = jax.random.normal(second_key, (ELEMS, NODE, NODE), jnp.float32) * (0.6 / NODE ** 0.5)
    spread = spread.at[:, node_ids, node_ids].set(diagonal)
    return spread.astype(jnp.bfloat16)


def draw_new_owner(key, part):
    device_count = ELEMS // E_DEV
    device_ids = jnp.arange(device_count + 1, dtype=jnp.int32)
    shifts = jax.random.randint(jax.random.fold_in(key, 23), (device_count + 1,), -MOVE, MOVE + 1)
    shifts = jnp.where(device_ids == 1, -MOVE, shifts)
    shifts = jnp.where(device_ids == 2, MOVE, shifts)
    shifts = jnp.where((device_ids == 0) | (device_ids == device_count), 0, shifts)
    cuts = device_ids * E_DEV + shifts
    element_ids = jnp.arange(ELEMS, dtype=jnp.int32)
    inner = cuts[1:device_count]
    owners = jnp.sum((element_ids[:, None] >= inner[None, :]).astype(jnp.int32), axis=1)
    return owners.astype(jnp.int32)


def draw_neighbors(key, part):
    first_key, second_key = jax.random.split(jax.random.fold_in(key, 37))
    distance = jax.random.randint(first_key, (ELEMS, 6), 1, REACH + 1)
    direction = 2 * jax.random.randint(second_key, (ELEMS, 6), 0, 2) - 1
    element_ids = jnp.arange(ELEMS, dtype=jnp.int32)[:, None]
    targets = element_ids + distance * direction
    targets = targets.at[REACH, 0].set(0)
    targets = targets.at[ELEMS - 1 - REACH, 1].set(ELEMS - 1)
    targets = targets.at[0, 2].set(-1)
    targets = jnp.where((targets < 0) | (targets >= ELEMS), -1, targets)
    return targets.astype(jnp.int32)


def place_ends(drawn, stream_key, low, largest):
    place = [jax.random.randint(jax.random.fold_in(stream_key, axis), (), 0, length) for axis, length in enumerate(drawn.shape)]
    widest = drawn.shape.index(max(drawn.shape))
    beside = place[:widest] + [(place[widest] + 1) % drawn.shape[widest]] + place[widest + 1:]
    return drawn.at[tuple(place)].set(low).at[tuple(beside)].set(largest)


def block_levels(key, extent, cuts, least, top_value):
    gain, own = 1.0, jax.random.fold_in(key, 6)
    for dim, parts in cuts:
        steps = jnp.exp(jax.random.uniform(jax.random.fold_in(own, dim), (parts,), jnp.float32, least / len(cuts), top_value / len(cuts)))
        gain = gain * jnp.repeat(steps, extent[dim] // parts).reshape([-1 if axis == dim else 1 for axis in range(len(extent))])
    return gain


def noise(key, shape, scale, bound, cuts=(), kind=jnp.bfloat16):
    result = scale * jax.random.normal(key, shape, jnp.float32)
    if cuts:
        result = result * block_levels(key, shape, cuts, -0.22, 0.18)
    return jnp.clip(result, -bound, bound).astype(kind)


def setup_inputs(seed: int = 0) -> dict:
    key_of = jax.random.split(jax.random.key(seed), 10)
    elem_state = noise(key_of[0], (ELEMS, VARS, NODE), 1.0, 6.0, ((0, 128),))
    mass_inverse = draw_mass_inverse(jax.random.fold_in(key_of[9], 71), 0)
    jacobian = noise(key_of[2], (ELEMS, NODE, NODE), NODE ** -0.5, 0.4375, ((0, 128),))
    elem_order = place_ends(jax.random.randint(key_of[3], (ELEMS,), 2, 6), jax.random.fold_in(key_of[3], 1), 2, 5).astype(jnp.int32)
    new_owner = draw_new_owner(jax.random.fold_in(key_of[9], 71), 0)
    neighbors = draw_neighbors(jax.random.fold_in(key_of[9], 71), 0)
    penalty = jnp.clip(jnp.exp(math.log(0.5) - 2.306499 * jax.random.uniform(key_of[6], (ELEMS, FACES), jnp.float32) ** block_levels(key_of[6], (ELEMS, FACES), ((0, 128),), -0.2, 0.2)), 0.049804688, 0.5).astype(jnp.bfloat16)
    closure_in = noise(key_of[7], (HID, VARS), VARS ** -0.5, 2.5)
    closure_out = noise(key_of[8], (VARS, HID), HID ** -0.5, 0.75)
    return dict(elem_state=elem_state, mass_inverse=mass_inverse, jacobian=jacobian, elem_order=elem_order, new_owner=new_owner, neighbors=neighbors, penalty=penalty, closure_in=closure_in, closure_out=closure_out)


def keep_mask(order_rows, node_count):
    limit = (order_rows + 1) ** 3
    node_ids = jnp.arange(node_count, dtype=jnp.int32)
    return (node_ids[None, :] < limit[:, None]).astype(jnp.float32)[:, None, :]


def reference(elem_state, mass_inverse, jacobian, elem_order, new_owner, neighbors, penalty, closure_in, closure_out):
    retained = keep_mask(elem_order, NODE)
    current = elem_state.astype(jnp.float32)
    mass_blocks = mass_inverse.reshape(N_DOM, E_DEV, NODE, NODE)
    jac_blocks = jacobian.reshape(N_DOM, E_DEV, NODE, NODE)
    near_ids = jnp.where(neighbors < 0, ELEMS, neighbors).astype(jnp.int32)
    for sweep_idx in range(SWEEPS):
        rounded = current.astype(jnp.bfloat16)

        def apply_mass(pair):
            tiles, values = pair
            return jnp.einsum('enm,evm->evn', tiles.astype(jnp.float32), values.astype(jnp.float32),
                              precision=lax.Precision.HIGHEST).astype(jnp.bfloat16)

        weighted = lax.map(apply_mass, (mass_blocks, rounded.reshape(N_DOM, E_DEV, VARS, NODE)))
        weighted = weighted.reshape(ELEMS, VARS, NODE)
        padded = jnp.concatenate([weighted, jnp.zeros((1, VARS, NODE), jnp.bfloat16)], axis=0)

        def update(group):
            tiles, own, near_idx, weights_face, values, prior, mask_rows = group
            beside = padded[near_idx]
            difference = beside.astype(jnp.float32) - own.astype(jnp.float32)[:, None]
            coupling = jnp.sum(weights_face.astype(jnp.float32)[:, :, None, None] * difference, axis=1)
            transport = jnp.einsum('enm,evn->evm', tiles.astype(jnp.float32), own.astype(jnp.float32),
                                   precision=lax.Precision.HIGHEST)
            hidden = jnp.tanh(jnp.einsum('hv,evn->ehn', closure_in.astype(jnp.float32), values.astype(jnp.float32),
                                         precision=lax.Precision.HIGHEST)).astype(jnp.bfloat16)
            closure = jnp.einsum('vh,ehn->evn', closure_out.astype(jnp.float32), hidden.astype(jnp.float32),
                                 precision=lax.Precision.HIGHEST)
            return (prior + transport + coupling + closure) * mask_rows

        current = lax.map(update, (jac_blocks,
                                   weighted.reshape(N_DOM, E_DEV, VARS, NODE),
                                   near_ids.reshape(N_DOM, E_DEV, FACES),
                                   penalty.reshape(N_DOM, E_DEV, FACES),
                                   rounded.reshape(N_DOM, E_DEV, VARS, NODE),
                                   current.reshape(N_DOM, E_DEV, VARS, NODE),
                                   retained.reshape(N_DOM, E_DEV, 1, NODE)))
        current = current.reshape(ELEMS, VARS, NODE)
    device_ids = jnp.arange(N_DOM, dtype=jnp.int32)
    counts = jnp.sum((new_owner[None, :] == device_ids[:, None]).astype(jnp.int32), axis=1)
    starts = jnp.cumsum(counts) - counts
    slots = jnp.arange(ELEMS, dtype=jnp.int32) - starts[new_owner]
    target_rows = (new_owner * CAP + slots).astype(jnp.int32)
    migrated = jnp.zeros((N_DOM * CAP, VARS, NODE), jnp.float32).at[target_rows].set(current)
    migrated_mass = jnp.zeros((N_DOM * CAP, NODE, NODE), jnp.bfloat16).at[target_rows].set(mass_inverse)
    migrated_jacobian = jnp.zeros((N_DOM * CAP, NODE, NODE), jnp.bfloat16).at[target_rows].set(jacobian)
    return (migrated, migrated_mass, migrated_jacobian)
```

```python
import functools

import jax
import jax.numpy as jnp
from jax import lax
from jax.experimental import pallas as pl
from jax.experimental.pallas import tpu as pltpu
from jax.sharding import PartitionSpec as P

SWEEPS = 2
SLOT = 8
MOVE = 8
REACH = 16
LANES = 128
NT = (((1,), (1,)), ((), ()))
NN = (((1,), (0,)), ((), ()))
F32 = jnp.float32
BF16 = jnp.bfloat16


def dot(a, b, dims=NN):
    return lax.dot_general(a, b, dims, preferred_element_type=F32)


def iota(shape, dim):
    return lax.broadcasted_iota(jnp.int32, shape, dim)


def sweep_kernel(
    count,
    state_hbm,
    mass_hbm,
    jac_hbm,
    order_hbm,
    owner_hbm,
    near_hbm,
    penalty_hbm,
    inner_hbm,
    outer_hbm,
    mass,
    jac,
    final,
    info,
    state,
    order,
    owners,
    near,
    penalty,
    inner,
    outer,
    current,
    rounded,
    weighted,
    added,
    keep,
    couple,
    target,
    share,
    first_layer,
    second_layer,
    load_sem,
    tile_sem,
    send_sem,
    recv_sem,
):
    me = lax.axis_index("dom")
    right = lax.rem(me + 1, count)
    left = lax.rem(me + count - 1, count)
    elems, nodes = mass_hbm.shape[0], mass_hbm.shape[2]
    rows = elems * SLOT
    edge = MOVE * SLOT
    halo = REACH * SLOT
    core = pl.ds(MOVE, elems)

    small = [
        pltpu.make_async_copy(src, dst, load_sem.at[i])
        for i, (src, dst) in enumerate(
            [
                (state_hbm, state),
                (order_hbm, order),
                (owner_hbm, owners.at[0]),
                (near_hbm, near),
                (penalty_hbm, penalty),
                (inner_hbm, inner),
                (outer_hbm, outer),
            ]
        )
    ]
    big = [
        pltpu.make_async_copy(mass_hbm, mass.at[core], tile_sem.at[0]),
        pltpu.make_async_copy(jac_hbm, jac.at[core], tile_sem.at[1]),
    ]
    for copy in small + big:
        copy.start()

    barrier = pltpu.get_barrier_semaphore()
    for neighbour in (left, right):
        pl.semaphore_signal(
            barrier, inc=1, device_id=(neighbour,), device_id_type=pl.DeviceIdType.MESH
        )
    pl.semaphore_wait(barrier, 2)

    def send(slot, src, dst, device):
        copy = pltpu.make_async_remote_copy(
            src_ref=src,
            dst_ref=dst,
            send_sem=send_sem.at[slot],
            recv_sem=recv_sem.at[slot],
            device_id=(device,),
            device_id_type=pl.DeviceIdType.MESH,
        )
        copy.start()
        return copy

    tail = pl.ds(elems - MOVE, MOVE)
    head = pl.ds(0, MOVE)
    beyond = pl.ds(MOVE + elems, MOVE)
    bulk = [
        send(0, owner_hbm, owners.at[1], right),
        send(1, owner_hbm, owners.at[2], left),
        send(2, mass_hbm.at[tail], mass.at[head], right),
        send(3, mass_hbm.at[head], mass.at[beyond], left),
        send(4, jac_hbm.at[tail], jac.at[head], right),
        send(5, jac_hbm.at[head], jac.at[beyond], left),
    ]

    for copy in small:
        copy.wait()

    row_of = iota((rows, elems), 0) - SLOT * iota((rows, elems), 1)
    current[...] = sum(
        dot((row_of == var).astype(F32).astype(BF16), state[var]) for var in range(state.shape[0])
    )

    spread = (iota((rows, elems), 0) // SLOT == iota((rows, elems), 1)).astype(F32).astype(BF16)
    base = me * elems - REACH
    local = jnp.where(near[...] < 0, -1, near[...] - base).astype(F32).astype(BF16)
    faces = near.shape[0]
    near_rows = dot(spread, local, NT)
    lane_var = (iota((rows, faces), 0) % SLOT).astype(F32)
    target[...] = near_rows * SLOT + lane_var
    share[...] = dot(spread, penalty[...], NT)
    orders = jnp.broadcast_to(order[...].astype(F32), (SLOT, elems)).astype(BF16)
    limit = dot(spread, orders, NT)[:, 0:1] + 1.0
    limit = limit * limit * limit
    keep[...] = (iota((rows, nodes), 1).astype(F32) < limit).astype(F32)

    span = couple.shape[2]
    step = 32

    def couple_rows(i, _):
        at = pl.ds(pl.multiple_of(i * step, step), step)
        cols = iota((step, span), 1).astype(F32)
        total = jnp.zeros((step, span), F32)
        for face in range(faces):
            hit = cols == target[at, face : face + 1]
            total = total + jnp.where(hit, share[at, face : face + 1], 0.0)
        high = total.astype(BF16)
        couple[0, at, :] = high
        couple[1, at, :] = (total - high.astype(F32)).astype(BF16)
        return 0

    lax.fori_loop(0, rows // step, couple_rows, 0)

    group = 4
    hid = inner.shape[1]
    variables = inner.shape[0]
    wide = group * SLOT
    tall = group * hid
    pick = (iota((variables, wide), 1) % SLOT == iota((variables, wide), 0)).astype(F32).astype(BF16)
    repeat = (iota((hid, tall), 1) % hid == iota((hid, tall), 0)).astype(F32).astype(BF16)
    tn = (((0,), (0,)), ((), ()))
    inner_wide = dot(inner[...], pick, tn).astype(BF16)
    inner_tall = dot(repeat, inner_wide, tn)
    same = iota((tall, wide), 0) // hid == iota((tall, wide), 1) // SLOT
    first_layer[...] = jnp.where(same, inner_tall, 0.0).astype(BF16)
    outer_wide = dot(outer[...], repeat).astype(BF16)
    outer_tall = dot(pick, outer_wide, tn)
    same = iota((wide, tall), 0) // SLOT == iota((wide, tall), 1) // hid
    second_layer[...] = jnp.where(same, outer_tall, 0.0).astype(BF16)

    pairs = elems // 2
    unroll = 4
    upper = iota((2 * SLOT, nodes), 0) < SLOT
    own = halo

    for sweep in range(SWEEPS):
        spot = weighted.at[sweep]
        rounded[...] = current[...].astype(BF16)
        if sweep == 0:
            big[0].wait()

        def weigh(i, _):
            for k in range(unroll):
                pair = i * unroll + k
                at = pl.ds(pl.multiple_of(pair * 2 * SLOT, 2 * SLOT), 2 * SLOT)
                values = rounded[at, :]
                one = dot(values, mass[MOVE + 2 * pair], NT)
                two = dot(values, mass[MOVE + 2 * pair + 1], NT)
                to = pl.ds(pl.multiple_of(own + pair * 2 * SLOT, 2 * SLOT), 2 * SLOT)
                spot[to, :] = jnp.where(upper, one, two).astype(BF16)
            return 0

        lax.fori_loop(0, pairs // unroll // 2, weigh, 0)
        to_left = send(
            6 + 2 * sweep, spot.at[pl.ds(own, halo)], spot.at[pl.ds(own + rows, halo)], left
        )
        lax.fori_loop(pairs // unroll // 2, pairs // unroll, weigh, 0)
        to_right = send(
            7 + 2 * sweep, spot.at[pl.ds(own + rows - halo, halo)], spot.at[pl.ds(0, halo)], right
        )

        def close(i, _):
            at = pl.ds(pl.multiple_of(i * wide, wide), wide)
            hidden = jnp.tanh(dot(first_layer[...], rounded[at, :])).astype(BF16)
            added[at, :] = dot(second_layer[...], hidden)
            return 0

        lax.fori_loop(0, rows // wide, close, 0)
        if sweep == 0:
            big[1].wait()

        def transport(i, _):
            for k in range(unroll):
                pair = i * unroll + k
                at = pl.ds(pl.multiple_of(pair * 2 * SLOT, 2 * SLOT), 2 * SLOT)
                frm = pl.ds(pl.multiple_of(own + pair * 2 * SLOT, 2 * SLOT), 2 * SLOT)
                values = spot[frm, :]
                one = dot(values, jac[MOVE + 2 * pair])
                two = dot(values, jac[MOVE + 2 * pair + 1])
                added[at, :] = added[at, :] + jnp.where(upper, one, two)
            return 0

        lax.fori_loop(0, pairs // unroll, transport, 0)
        to_left.wait()
        to_right.wait()
        block = 64

        def finish(i, _):
            at = pl.ds(pl.multiple_of(i * block, block), block)
            frm = pl.ds(pl.multiple_of(own + i * block, block), block)
            beside = dot(couple[0, at, :], spot[...]) + dot(couple[1, at, :], spot[...])
            total = jnp.sum(share[at, :], axis=1, keepdims=True)
            coupling = beside - total * spot[frm, :].astype(F32)
            value = (current[at, :] + added[at, :] + coupling) * keep[at, :]
            if sweep == SWEEPS - 1:
                to = pl.ds(pl.multiple_of(edge + i * block, block), block)
                final[0, to, :] = value[:, :LANES]
                final[1, to, 0 : nodes - LANES] = value[:, LANES:]
            else:
                current[at, :] = value
            return 0

        lax.fori_loop(0, rows // block, finish, 0)

    last = [
        send(10, final.at[:, pl.ds(rows, edge)], final.at[:, pl.ds(0, edge)], right),
        send(11, final.at[:, pl.ds(edge, edge)], final.at[:, pl.ds(edge + rows, edge)], left),
    ]
    for copy in bulk[:2]:
        copy.wait()

    def tally(hits):
        return jnp.sum(hits.astype(F32), axis=1, keepdims=True)

    from_left = tally(owners[1] == me)
    from_right = tally(owners[2] == me)
    stay = tally(owners[0] == me)
    gone = tally(owners[0] == me - 1)
    filled = stay + from_left + from_right
    leading = gone - from_left + MOVE
    line = iota(info.shape, 0)
    info[...] = jnp.where(line == 0, leading, filled)
    for copy in bulk[2:] + last:
        copy.wait()


def place_kernel(mass, jac, final, info, out_mass, out_jac, out_final, zeros, sem):
    leading = jnp.max(info[0:1, :]).astype(jnp.int32)
    filled = jnp.max(info[1:2, :]).astype(jnp.int32)
    slots = out_mass.shape[0]
    always = slots // 3
    group = zeros.shape[0]
    for src, dst in ((mass, out_mass), (jac, out_jac)):
        pltpu.make_async_copy(
            src.at[pl.ds(leading, always)], dst.at[pl.ds(0, always)], sem
        ).start()
    zeros[...] = jnp.zeros(zeros.shape, zeros.dtype)
    for src, dst in ((mass, out_mass), (jac, out_jac)):
        for start in range(always, slots, group):
            to = dst.at[pl.ds(start, group)]

            @pl.when(filled >= start + group)
            def _():
                pltpu.make_async_copy(src.at[pl.ds(leading + start, group)], to, sem).start()

            @pl.when(filled <= start)
            def _():
                pltpu.make_async_copy(zeros, to, sem).start()

            @pl.when((filled > start) & (filled < start + group))
            def _():
                def live(i, _):
                    pltpu.make_async_copy(src.at[leading + i], dst.at[i], sem).start()
                    return 0

                def dead(i, _):
                    pltpu.make_async_copy(zeros.at[0], dst.at[i], sem).start()
                    return 0

                lax.fori_loop(start, filled, live, 0)
                lax.fori_loop(filled, start + group, dead, 0)

    variables = out_final.shape[0]
    nodes = out_final.shape[2]
    alive = iota((slots, LANES), 0) < filled
    for var in range(variables):
        at = pl.ds(leading * SLOT + var, slots, stride=SLOT)
        out_final[var, :, 0:LANES] = jnp.where(alive, final[0, at, :], 0.0)
        out_final[var, :, LANES:nodes] = jnp.where(alive, final[1, at, :], 0.0)[:, : nodes - LANES]
    for dst in (out_mass, out_jac):
        pltpu.make_async_copy(dst, dst, sem).wait()


def shards(
    elem_state,
    mass_inverse,
    jacobian,
    elem_order,
    new_owner,
    neighbors,
    penalty,
    closure_in,
    closure_out,
):
    elems, variables, nodes = elem_state.shape
    hid = closure_in.shape[0]
    faces = neighbors.shape[1]
    count = lax.axis_size("dom")
    slots = elems + 2 * MOVE
    rows = elems * SLOT
    span = rows + 2 * REACH * SLOT
    anywhere = pl.BlockSpec(memory_space=pl.ANY)
    near_by = pl.BlockSpec(memory_space=pltpu.VMEM)
    dma = pltpu.SemaphoreType.DMA
    mass, jac, final, info = pl.pallas_call(
        functools.partial(sweep_kernel, count),
        out_shape=(
            pltpu.VMEM((slots, nodes, nodes), BF16),
            pltpu.VMEM((slots, nodes, nodes), BF16),
            pltpu.VMEM((2, (slots + 2 * MOVE) * SLOT, LANES), F32),
            pltpu.VMEM((8, 128), F32),
        ),
        in_specs=[anywhere] * 9,
        out_specs=(near_by,) * 4,
        scratch_shapes=[
            pltpu.VMEM((variables, elems, nodes), BF16),
            pltpu.VMEM((1, elems), jnp.int32),
            pltpu.VMEM((3, 1, elems), jnp.int32),
            pltpu.VMEM((faces, elems), jnp.int32),
            pltpu.VMEM((faces, elems), BF16),
            pltpu.VMEM((variables, hid), BF16),
            pltpu.VMEM((variables, hid), BF16),
            pltpu.VMEM((rows, nodes), F32),
            pltpu.VMEM((rows, nodes), BF16),
            pltpu.VMEM((SWEEPS, span, nodes), BF16),
            pltpu.VMEM((rows, nodes), F32),
            pltpu.VMEM((rows, nodes), F32),
            pltpu.VMEM((2, rows, span), BF16),
            pltpu.VMEM((rows, faces), F32),
            pltpu.VMEM((rows, faces), F32),
            pltpu.VMEM((4 * hid, 4 * SLOT), BF16),
            pltpu.VMEM((4 * SLOT, 4 * hid), BF16),
            dma((7,)),
            dma((2,)),
            dma((12,)),
            dma((12,)),
        ],
        compiler_params=pltpu.CompilerParams(
            collective_id=0, has_side_effects=True, vmem_limit_bytes=24 * 2**20
        ),
        name="sweeps",
    )(
        jnp.transpose(elem_state, (1, 0, 2)),
        mass_inverse,
        jacobian,
        elem_order.reshape(1, elems),
        new_owner.reshape(1, elems),
        neighbors.T,
        penalty.T,
        closure_in.T,
        closure_out,
    )
    out_mass, out_jac, out_final = pl.pallas_call(
        place_kernel,
        out_shape=(
            jax.ShapeDtypeStruct((slots, nodes, nodes), BF16),
            jax.ShapeDtypeStruct((slots, nodes, nodes), BF16),
            jax.ShapeDtypeStruct((variables, slots, nodes), F32),
        ),
        in_specs=[near_by] * 4,
        out_specs=(anywhere, anywhere, near_by),
        scratch_shapes=[pltpu.VMEM((8, nodes, nodes), BF16), dma],
        compiler_params=pltpu.CompilerParams(vmem_limit_bytes=24 * 2**20),
        name="place",
    )(mass, jac, final, info)
    return (jnp.transpose(out_final, (1, 0, 2)), out_mass, out_jac)


def solution(mesh):
    placed = (
        P("dom", None, None),
        P("dom", None, None),
        P("dom", None, None),
        P("dom"),
        P("dom"),
        P("dom", None),
        P("dom", None),
        P(),
        P(),
    )
    return jax.shard_map(
        shards,
        mesh=mesh,
        in_specs=placed,
        out_specs=(P("dom", None, None), P("dom", None, None), P("dom", None, None)),
        check_vma=False,
    )
```

```python
import functools

import jax
import jax.numpy as jnp
from jax import lax
from jax.experimental import pallas as pl
from jax.experimental.pallas import tpu as pltpu
from jax.sharding import PartitionSpec as P

SWEEPS = 2
SLOT = 8
MOVE = 8
REACH = 16
LANES = 128
NT = (((1,), (1,)), ((), ()))
NN = (((1,), (0,)), ((), ()))
F32 = jnp.float32
BF16 = jnp.bfloat16


def dot(a, b, dims=NN):
    return lax.dot_general(a, b, dims, preferred_element_type=F32)


def iota(shape, dim):
    return lax.broadcasted_iota(jnp.int32, shape, dim)


def sweep_kernel(
    count,
    state_hbm,
    mass_hbm,
    jac_hbm,
    order_hbm,
    owner_hbm,
    near_hbm,
    penalty_hbm,
    inner_hbm,
    outer_hbm,
    mass,
    jac,
    final,
    info,
    state,
    order,
    owners,
    near,
    penalty,
    inner,
    outer,
    current,
    rounded,
    weighted,
    added,
    keep,
    couple,
    target,
    share,
    first_layer,
    second_layer,
    load_sem,
    tile_sem,
    send_sem,
    recv_sem,
):
    me = lax.axis_index("dom")
    right = lax.rem(me + 1, count)
    left = lax.rem(me + count - 1, count)
    elems, nodes = mass_hbm.shape[0], mass_hbm.shape[2]
    rows = elems * SLOT
    edge = MOVE * SLOT
    halo = REACH * SLOT
    core = pl.ds(MOVE, elems)

    small = [
        pltpu.make_async_copy(src, dst, load_sem.at[i])
        for i, (src, dst) in enumerate(
            [
                (state_hbm, state),
                (order_hbm, order),
                (owner_hbm, owners.at[0]),
                (near_hbm, near),
                (penalty_hbm, penalty),
                (inner_hbm, inner),
                (outer_hbm, outer),
            ]
        )
    ]
    big = [
        pltpu.make_async_copy(mass_hbm, mass.at[core], tile_sem.at[0]),
        pltpu.make_async_copy(jac_hbm, jac.at[core], tile_sem.at[1]),
    ]
    for copy in small + big:
        copy.start()

    has_left = me > 0
    has_right = me < count - 1
    barrier = pltpu.get_barrier_semaphore()

    def greet(device):
        pl.semaphore_signal(
            barrier, inc=1, device_id=(device,), device_id_type=pl.DeviceIdType.MESH
        )

    @pl.when(has_left)
    def _():
        greet(me - 1)

    @pl.when(has_right)
    def _():
        greet(me + 1)

    pl.semaphore_wait(barrier, has_left.astype(jnp.int32) + has_right.astype(jnp.int32))

    def sender(slot, src, dst, device):
        return pltpu.make_async_remote_copy(
            src_ref=src,
            dst_ref=dst,
            send_sem=send_sem.at[slot],
            recv_sem=recv_sem.at[slot],
            device_id=(device,),
            device_id_type=pl.DeviceIdType.MESH,
        )

    class ToRight:
        def __init__(self, slot, src, dst):
            self.copy = sender(slot, src, dst, right)
            pl.when(has_right)(self.copy.start)

        def wait(self):
            pl.when(has_right)(self.copy.wait_send)
            pl.when(has_left)(self.copy.wait_recv)

    class ToLeft:
        def __init__(self, slot, src, dst):
            self.copy = sender(slot, src, dst, left)
            pl.when(has_left)(self.copy.start)

        def wait(self):
            pl.when(has_left)(self.copy.wait_send)
            pl.when(has_right)(self.copy.wait_recv)

    tail = pl.ds(elems - MOVE, MOVE)
    head = pl.ds(0, MOVE)
    beyond = pl.ds(MOVE + elems, MOVE)
    bulk = [
        ToRight(0, owner_hbm, owners.at[1]),
        ToLeft(1, owner_hbm, owners.at[2]),
        ToRight(2, mass_hbm.at[tail], mass.at[head]),
        ToLeft(3, mass_hbm.at[head], mass.at[beyond]),
        ToRight(4, jac_hbm.at[tail], jac.at[head]),
        ToLeft(5, jac_hbm.at[head], jac.at[beyond]),
    ]

    @pl.when(jnp.logical_not(has_left))
    def _():
        for sweep in range(SWEEPS):
            weighted[sweep, 0:halo, :] = jnp.zeros((halo, nodes), BF16)
        owners[1] = jnp.full((1, elems), -1, jnp.int32)

    @pl.when(jnp.logical_not(has_right))
    def _():
        for sweep in range(SWEEPS):
            weighted[sweep, halo + rows : 2 * halo + rows, :] = jnp.zeros((halo, nodes), BF16)
        owners[2] = jnp.full((1, elems), -1, jnp.int32)

    for copy in small:
        copy.wait()

    row_of = iota((rows, elems), 0) - SLOT * iota((rows, elems), 1)
    current[...] = sum(
        dot((row_of == var).astype(F32).astype(BF16), state[var]) for var in range(state.shape[0])
    )

    spread = (iota((rows, elems), 0) // SLOT == iota((rows, elems), 1)).astype(F32).astype(BF16)
    base = me * elems - REACH
    local = jnp.where(near[...] < 0, -1, near[...] - base).astype(F32).astype(BF16)
    faces = near.shape[0]
    near_rows = dot(spread, local, NT)
    lane_var = (iota((rows, faces), 0) % SLOT).astype(F32)
    target[...] = near_rows * SLOT + lane_var
    share[...] = dot(spread, penalty[...], NT)
    orders = jnp.broadcast_to(order[...].astype(F32), (SLOT, elems)).astype(BF16)
    limit = dot(spread, orders, NT)[:, 0:1] + 1.0
    limit = limit * limit * limit
    keep[...] = (iota((rows, nodes), 1).astype(F32) < limit).astype(F32)

    span = couple.shape[2]
    step = 32

    def couple_rows(i, _):
        at = pl.ds(pl.multiple_of(i * step, step), step)
        cols = iota((step, span), 1).astype(F32)
        total = jnp.zeros((step, span), F32)
        for face in range(faces):
            hit = cols == target[at, face : face + 1]
            total = total + jnp.where(hit, share[at, face : face + 1], 0.0)
        high = total.astype(BF16)
        couple[0, at, :] = high
        couple[1, at, :] = (total - high.astype(F32)).astype(BF16)
        return 0

    lax.fori_loop(0, rows // step, couple_rows, 0)

    group = 4
    hid = inner.shape[1]
    variables = inner.shape[0]
    wide = group * SLOT
    tall = group * hid
    pick = (iota((variables, wide), 1) % SLOT == iota((variables, wide), 0)).astype(F32).astype(BF16)
    repeat = (iota((hid, tall), 1) % hid == iota((hid, tall), 0)).astype(F32).astype(BF16)
    tn = (((0,), (0,)), ((), ()))
    inner_wide = dot(inner[...], pick, tn).astype(BF16)
    inner_tall = dot(repeat, inner_wide, tn)
    same = iota((tall, wide), 0) // hid == iota((tall, wide), 1) // SLOT
    first_layer[...] = jnp.where(same, inner_tall, 0.0).astype(BF16)
    outer_wide = dot(outer[...], repeat).astype(BF16)
    outer_tall = dot(pick, outer_wide, tn)
    same = iota((wide, tall), 0) // SLOT == iota((wide, tall), 1) // hid
    second_layer[...] = jnp.where(same, outer_tall, 0.0).astype(BF16)

    pairs = elems // 2
    unroll = 4
    upper = iota((2 * SLOT, nodes), 0) < SLOT
    own = halo

    for sweep in range(SWEEPS):
        spot = weighted.at[sweep]
        rounded[...] = current[...].astype(BF16)
        if sweep == 0:
            big[0].wait()

        def weigh(i, _):
            for k in range(unroll):
                pair = i * unroll + k
                at = pl.ds(pl.multiple_of(pair * 2 * SLOT, 2 * SLOT), 2 * SLOT)
                values = rounded[at, :]
                one = dot(values, mass[MOVE + 2 * pair], NT)
                two = dot(values, mass[MOVE + 2 * pair + 1], NT)
                to = pl.ds(pl.multiple_of(own + pair * 2 * SLOT, 2 * SLOT), 2 * SLOT)
                spot[to, :] = jnp.where(upper, one, two).astype(BF16)
            return 0

        lax.fori_loop(0, pairs // unroll // 2, weigh, 0)
        to_left = ToLeft(
            6 + 2 * sweep, spot.at[pl.ds(own, halo)], spot.at[pl.ds(own + rows, halo)]
        )
        lax.fori_loop(pairs // unroll // 2, pairs // unroll, weigh, 0)
        to_right = ToRight(
            7 + 2 * sweep, spot.at[pl.ds(own + rows - halo, halo)], spot.at[pl.ds(0, halo)]
        )

        def close(i, _):
            at = pl.ds(pl.multiple_of(i * wide, wide), wide)
            hidden = jnp.tanh(dot(first_layer[...], rounded[at, :])).astype(BF16)
            added[at, :] = dot(second_layer[...], hidden)
            return 0

        lax.fori_loop(0, rows // wide, close, 0)
        if sweep == 0:
            big[1].wait()

        def transport(i, _):
            for k in range(unroll):
                pair = i * unroll + k
                at = pl.ds(pl.multiple_of(pair * 2 * SLOT, 2 * SLOT), 2 * SLOT)
                frm = pl.ds(pl.multiple_of(own + pair * 2 * SLOT, 2 * SLOT), 2 * SLOT)
                values = spot[frm, :]
                one = dot(values, jac[MOVE + 2 * pair])
                two = dot(values, jac[MOVE + 2 * pair + 1])
                added[at, :] = added[at, :] + jnp.where(upper, one, two)
            return 0

        lax.fori_loop(0, pairs // unroll, transport, 0)
        to_left.wait()
        to_right.wait()
        block = 64

        def finish(i, _):
            at = pl.ds(pl.multiple_of(i * block, block), block)
            frm = pl.ds(pl.multiple_of(own + i * block, block), block)
            beside = dot(couple[0, at, :], spot[...]) + dot(couple[1, at, :], spot[...])
            total = jnp.sum(share[at, :], axis=1, keepdims=True)
            coupling = beside - total * spot[frm, :].astype(F32)
            value = (current[at, :] + added[at, :] + coupling) * keep[at, :]
            if sweep == SWEEPS - 1:
                to = pl.ds(pl.multiple_of(edge + i * block, block), block)
                final[0, to, :] = value[:, :LANES]
                final[1, to, 0 : nodes - LANES] = value[:, LANES:]
            else:
                current[at, :] = value
            return 0

        lax.fori_loop(0, rows // block, finish, 0)

    last = [
        ToRight(10, final.at[:, pl.ds(rows, edge)], final.at[:, pl.ds(0, edge)]),
        ToLeft(11, final.at[:, pl.ds(edge, edge)], final.at[:, pl.ds(edge + rows, edge)]),
    ]
    for copy in bulk[:2]:
        copy.wait()

    def tally(hits):
        return jnp.sum(hits.astype(F32), axis=1, keepdims=True)

    from_left = tally(owners[1] == me)
    from_right = tally(owners[2] == me)
    stay = tally(owners[0] == me)
    gone = tally(owners[0] == me - 1)
    filled = stay + from_left + from_right
    leading = gone - from_left + MOVE
    line = iota(info.shape, 0)
    info[...] = jnp.where(line == 0, leading, filled)
    for copy in bulk[2:] + last:
        copy.wait()


def place_kernel(mass, jac, final, info, out_mass, out_jac, out_final, zeros, sem):
    leading = jnp.max(info[0:1, :]).astype(jnp.int32)
    filled = jnp.max(info[1:2, :]).astype(jnp.int32)
    slots = out_mass.shape[0]
    always = slots // 3
    group = zeros.shape[0]
    for src, dst in ((mass, out_mass), (jac, out_jac)):
        pltpu.make_async_copy(
            src.at[pl.ds(leading, always)], dst.at[pl.ds(0, always)], sem
        ).start()
    zeros[...] = jnp.zeros(zeros.shape, zeros.dtype)
    for src, dst in ((mass, out_mass), (jac, out_jac)):
        for start in range(always, slots, group):
            to = dst.at[pl.ds(start, group)]

            @pl.when(filled >= start + group)
            def _():
                pltpu.make_async_copy(src.at[pl.ds(leading + start, group)], to, sem).start()

            @pl.when(filled <= start)
            def _():
                pltpu.make_async_copy(zeros, to, sem).start()

            @pl.when((filled > start) & (filled < start + group))
            def _():
                def live(i, _):
                    pltpu.make_async_copy(src.at[leading + i], dst.at[i], sem).start()
                    return 0

                def dead(i, _):
                    pltpu.make_async_copy(zeros.at[0], dst.at[i], sem).start()
                    return 0

                lax.fori_loop(start, filled, live, 0)
                lax.fori_loop(filled, start + group, dead, 0)

    variables = out_final.shape[0]
    nodes = out_final.shape[2]
    alive = iota((slots, LANES), 0) < filled
    for var in range(variables):
        at = pl.ds(leading * SLOT + var, slots, stride=SLOT)
        out_final[var, :, 0:LANES] = jnp.where(alive, final[0, at, :], 0.0)
        out_final[var, :, LANES:nodes] = jnp.where(alive, final[1, at, :], 0.0)[:, : nodes - LANES]
    for dst in (out_mass, out_jac):
        pltpu.make_async_copy(dst, dst, sem).wait()


def shards(
    elem_state,
    mass_inverse,
    jacobian,
    elem_order,
    new_owner,
    neighbors,
    penalty,
    closure_in,
    closure_out,
):
    elems, variables, nodes = elem_state.shape
    hid = closure_in.shape[0]
    faces = neighbors.shape[1]
    count = lax.axis_size("dom")
    slots = elems + 2 * MOVE
    rows = elems * SLOT
    span = rows + 2 * REACH * SLOT
    operands = (
        jnp.transpose(elem_state, (1, 0, 2)),
        mass_inverse,
        jacobian,
        elem_order.reshape(1, elems),
        new_owner.reshape(1, elems),
        neighbors.T,
        penalty.T,
        closure_in.T,
        closure_out,
    )
    anywhere = pl.BlockSpec(memory_space=pltpu.HBM)
    near_by = pl.BlockSpec(memory_space=pltpu.VMEM)
    dma = pltpu.SemaphoreType.DMA
    mass, jac, final, info = pl.pallas_call(
        functools.partial(sweep_kernel, count),
        out_shape=(
            pltpu.VMEM((slots, nodes, nodes), BF16),
            pltpu.VMEM((slots, nodes, nodes), BF16),
            pltpu.VMEM((2, (slots + 2 * MOVE) * SLOT, LANES), F32),
            pltpu.VMEM((8, 128), F32),
        ),
        in_specs=[anywhere] * 9,
        out_specs=(near_by,) * 4,
        scratch_shapes=[
            pltpu.VMEM((variables, elems, nodes), BF16),
            pltpu.VMEM((1, elems), jnp.int32),
            pltpu.VMEM((3, 1, elems), jnp.int32),
            pltpu.VMEM((faces, elems), jnp.int32),
            pltpu.VMEM((faces, elems), BF16),
            pltpu.VMEM((variables, hid), BF16),
            pltpu.VMEM((variables, hid), BF16),
            pltpu.VMEM((rows, nodes), F32),
            pltpu.VMEM((rows, nodes), BF16),
            pltpu.VMEM((SWEEPS, span, nodes), BF16),
            pltpu.VMEM((rows, nodes), F32),
            pltpu.VMEM((rows, nodes), F32),
            pltpu.VMEM((2, rows, span), BF16),
            pltpu.VMEM((rows, faces), F32),
            pltpu.VMEM((rows, faces), F32),
            pltpu.VMEM((4 * hid, 4 * SLOT), BF16),
            pltpu.VMEM((4 * SLOT, 4 * hid), BF16),
            dma((7,)),
            dma((2,)),
            dma((12,)),
            dma((12,)),
        ],
        compiler_params=pltpu.CompilerParams(
            collective_id=0, has_side_effects=True, vmem_limit_bytes=24 * 2**20
        ),
        name="sweeps",
    )(*(pltpu.with_memory_space_constraint(operand, pltpu.HBM) for operand in operands))
    out_mass, out_jac, out_final = pl.pallas_call(
        place_kernel,
        out_shape=(
            jax.ShapeDtypeStruct((slots, nodes, nodes), BF16),
            jax.ShapeDtypeStruct((slots, nodes, nodes), BF16),
            jax.ShapeDtypeStruct((variables, slots, nodes), F32),
        ),
        in_specs=[near_by] * 4,
        out_specs=(anywhere, anywhere, near_by),
        scratch_shapes=[pltpu.VMEM((8, nodes, nodes), BF16), dma],
        compiler_params=pltpu.CompilerParams(vmem_limit_bytes=24 * 2**20),
        name="place",
    )(mass, jac, final, info)
    return (jnp.transpose(out_final, (1, 0, 2)), out_mass, out_jac)


def solution(mesh):
    placed = (
        P("dom", None, None),
        P("dom", None, None),
        P("dom", None, None),
        P("dom"),
        P("dom"),
        P("dom", None),
        P("dom", None),
        P(),
        P(),
    )
    return jax.shard_map(
        shards,
        mesh=mesh,
        in_specs=placed,
        out_specs=(P("dom", None, None), P("dom", None, None), P("dom", None, None)),
        check_vma=False,
    )
```

```python
import functools

import jax
import jax.numpy as jnp
from jax import lax
from jax.experimental import pallas as pl
from jax.experimental.pallas import tpu as pltpu
from jax.sharding import PartitionSpec as P

SWEEPS = 2
SLOT = 8
MOVE = 8
REACH = 16
LANES = 128
SCHEDULE = (
    ((0, 0, 3),),
    ((0, 3, 5), (1, 0, 1)),
    ((1, 1, 4),),
    ((1, 5, 3),),
)
SENDS = 8 + 2 * sum(len(part) for part in SCHEDULE)
CLOSE = 2
NT = (((1,), (1,)), ((), ()))
NN = (((1,), (0,)), ((), ()))
F32 = jnp.float32
BF16 = jnp.bfloat16


def dot(a, b, dims=NN):
    return lax.dot_general(a, b, dims, preferred_element_type=F32)


def iota(shape, dim):
    return lax.broadcasted_iota(jnp.int32, shape, dim)


def sweep_kernel(
    count,
    state_hbm,
    mass_hbm,
    jac_hbm,
    order_hbm,
    owner_hbm,
    near_hbm,
    penalty_hbm,
    inner_hbm,
    outer_hbm,
    mass,
    jac,
    final,
    info,
    state,
    order,
    owners,
    near,
    penalty,
    inner,
    outer,
    current,
    rounded,
    weighted,
    added,
    keep,
    couple,
    target,
    share,
    first_layer,
    second_layer,
    load_sem,
    tile_sem,
    send_sem,
    recv_sem,
):
    me = lax.axis_index("dom")
    right = lax.rem(me + 1, count)
    left = lax.rem(me + count - 1, count)
    elems, nodes = mass_hbm.shape[0], mass_hbm.shape[2]
    rows = elems * SLOT
    edge = MOVE * SLOT
    halo = REACH * SLOT
    core = pl.ds(MOVE, elems)

    small = [
        pltpu.make_async_copy(src, dst, load_sem.at[i])
        for i, (src, dst) in enumerate(
            [
                (state_hbm, state),
                (order_hbm, order),
                (owner_hbm, owners.at[0]),
                (near_hbm, near),
                (penalty_hbm, penalty),
                (inner_hbm, inner),
                (outer_hbm, outer),
            ]
        )
    ]
    half = elems // 2
    mass_load = [
        pltpu.make_async_copy(
            mass_hbm.at[pl.ds(i * half, half)],
            mass.at[pl.ds(MOVE + i * half, half)],
            tile_sem.at[i],
        )
        for i in range(2)
    ]
    jac_load = pltpu.make_async_copy(jac_hbm, jac.at[core], tile_sem.at[2])
    for copy in small + mass_load + [jac_load]:
        copy.start()

    has_left = me > 0
    has_right = me < count - 1
    barrier = pltpu.get_barrier_semaphore()

    def greet(device):
        pl.semaphore_signal(
            barrier, inc=1, device_id=(device,), device_id_type=pl.DeviceIdType.MESH
        )

    @pl.when(has_left)
    def _():
        greet(me - 1)

    @pl.when(has_right)
    def _():
        greet(me + 1)

    pl.semaphore_wait(barrier, has_left.astype(jnp.int32) + has_right.astype(jnp.int32))

    def sender(slot, src, dst, device):
        return pltpu.make_async_remote_copy(
            src_ref=src,
            dst_ref=dst,
            send_sem=send_sem.at[slot],
            recv_sem=recv_sem.at[slot],
            device_id=(device,),
            device_id_type=pl.DeviceIdType.MESH,
        )

    class ToRight:
        def __init__(self, slot, src, dst):
            self.copy = sender(slot, src, dst, right)
            pl.when(has_right)(self.copy.start)

        def wait(self):
            pl.when(has_right)(self.copy.wait_send)
            pl.when(has_left)(self.copy.wait_recv)

    class ToLeft:
        def __init__(self, slot, src, dst):
            self.copy = sender(slot, src, dst, left)
            pl.when(has_left)(self.copy.start)

        def wait(self):
            pl.when(has_left)(self.copy.wait_send)
            pl.when(has_right)(self.copy.wait_recv)

    meta = [ToRight(0, owner_hbm, owners.at[1]), ToLeft(1, owner_hbm, owners.at[2])]
    bulk = []

    def tiles(phase):
        for which, start, size in SCHEDULE[phase]:
            src, dst = ((mass_hbm, mass), (jac_hbm, jac))[which]
            slot = 8 + len(bulk)
            bulk.append(
                ToRight(
                    slot,
                    src.at[pl.ds(elems - MOVE + start, size)],
                    dst.at[pl.ds(start, size)],
                )
            )
            bulk.append(
                ToLeft(
                    slot + 1,
                    src.at[pl.ds(start, size)],
                    dst.at[pl.ds(MOVE + elems + start, size)],
                )
            )

    tiles(0)

    @pl.when(jnp.logical_not(has_left))
    def _():
        for sweep in range(SWEEPS):
            weighted[sweep, 0:halo, :] = jnp.zeros((halo, nodes), BF16)
        owners[1] = jnp.full((1, elems), -1, jnp.int32)

    @pl.when(jnp.logical_not(has_right))
    def _():
        for sweep in range(SWEEPS):
            weighted[sweep, halo + rows : 2 * halo + rows, :] = jnp.zeros((halo, nodes), BF16)
        owners[2] = jnp.full((1, elems), -1, jnp.int32)

    small[0].wait()

    row_of = iota((rows, elems), 0) - SLOT * iota((rows, elems), 1)
    current[...] = sum(
        dot((row_of == var).astype(F32).astype(BF16), state[var]) for var in range(state.shape[0])
    )

    group = 4
    hid = inner.shape[1]
    variables = inner.shape[0]
    wide = group * SLOT
    tall = group * hid
    def prepare():
        for copy in small[1:]:
            copy.wait()

        spread = (iota((rows, elems), 0) // SLOT == iota((rows, elems), 1)).astype(F32).astype(BF16)
        base = me * elems - REACH
        local = jnp.where(near[...] < 0, -1, near[...] - base).astype(F32).astype(BF16)
        faces = near.shape[0]
        near_rows = dot(spread, local, NT)
        lane_var = (iota((rows, faces), 0) % SLOT).astype(F32)
        target[...] = near_rows * SLOT + lane_var
        share[...] = dot(spread, penalty[...], NT)
        orders = jnp.broadcast_to(order[...].astype(F32), (SLOT, elems)).astype(BF16)
        limit = dot(spread, orders, NT)[:, 0:1] + 1.0
        limit = limit * limit * limit
        keep[...] = (iota((rows, nodes), 1).astype(F32) < limit).astype(F32)

        span = couple.shape[2]
        step = 32

        def couple_rows(i, _):
            at = pl.ds(pl.multiple_of(i * step, step), step)
            cols = iota((step, span), 1).astype(F32)
            total = jnp.zeros((step, span), F32)
            for face in range(faces):
                hit = cols == target[at, face : face + 1]
                total = total + jnp.where(hit, share[at, face : face + 1], 0.0)
            high = total.astype(BF16)
            couple[0, at, :] = high
            couple[1, at, :] = (total - high.astype(F32)).astype(BF16)
            return 0

        lax.fori_loop(0, rows // step, couple_rows, 0)

        pick = (iota((variables, wide), 1) % SLOT == iota((variables, wide), 0)).astype(F32).astype(BF16)
        repeat = (iota((hid, tall), 1) % hid == iota((hid, tall), 0)).astype(F32).astype(BF16)
        tn = (((0,), (0,)), ((), ()))
        inner_wide = dot(inner[...], pick, tn).astype(BF16)
        inner_tall = dot(repeat, inner_wide, tn)
        same = iota((tall, wide), 0) // hid == iota((tall, wide), 1) // SLOT
        first_layer[...] = jnp.where(same, inner_tall, 0.0).astype(BF16)
        outer_wide = dot(outer[...], repeat).astype(BF16)
        outer_tall = dot(pick, outer_wide, tn)
        same = iota((wide, tall), 0) // SLOT == iota((wide, tall), 1) // hid
        second_layer[...] = jnp.where(same, outer_tall, 0.0).astype(BF16)

    pairs = elems // 2
    unroll = 4
    upper = iota((2 * SLOT, nodes), 0) < SLOT
    own = halo

    for sweep in range(SWEEPS):
        spot = weighted.at[sweep]
        rounded[...] = current[...].astype(BF16)
        if sweep == 0:
            mass_load[0].wait()

        def weigh(i, _):
            for k in range(unroll):
                pair = i * unroll + k
                at = pl.ds(pl.multiple_of(pair * 2 * SLOT, 2 * SLOT), 2 * SLOT)
                values = rounded[at, :]
                one = dot(values, mass[MOVE + 2 * pair], NT)
                two = dot(values, mass[MOVE + 2 * pair + 1], NT)
                to = pl.ds(pl.multiple_of(own + pair * 2 * SLOT, 2 * SLOT), 2 * SLOT)
                spot[to, :] = jnp.where(upper, one, two).astype(BF16)
            return 0

        lax.fori_loop(0, pairs // unroll // 2, weigh, 0)
        to_left = ToLeft(
            2 + 2 * sweep, spot.at[pl.ds(own, halo)], spot.at[pl.ds(own + rows, halo)]
        )
        if sweep == 0:
            mass_load[1].wait()
        lax.fori_loop(pairs // unroll // 2, pairs // unroll, weigh, 0)
        to_right = ToRight(
            3 + 2 * sweep, spot.at[pl.ds(own + rows - halo, halo)], spot.at[pl.ds(0, halo)]
        )

        tiles(sweep + 1)
        if sweep == 0:
            prepare()

        def close(i, _):
            ats = [
                pl.ds(pl.multiple_of((i * CLOSE + k) * wide, wide), wide) for k in range(CLOSE)
            ]
            inputs = [dot(first_layer[...], rounded[at, :]) for at in ats]
            hidden = [jnp.tanh(value).astype(BF16) for value in inputs]
            for at, value in zip(ats, hidden):
                added[at, :] = dot(second_layer[...], value)
            return 0

        lax.fori_loop(0, rows // wide // CLOSE, close, 0)
        if sweep == 0:
            jac_load.wait()

        def transport(i, _):
            for k in range(unroll):
                pair = i * unroll + k
                at = pl.ds(pl.multiple_of(pair * 2 * SLOT, 2 * SLOT), 2 * SLOT)
                frm = pl.ds(pl.multiple_of(own + pair * 2 * SLOT, 2 * SLOT), 2 * SLOT)
                values = spot[frm, :]
                one = dot(values, jac[MOVE + 2 * pair])
                two = dot(values, jac[MOVE + 2 * pair + 1])
                added[at, :] = added[at, :] + jnp.where(upper, one, two)
            return 0

        lax.fori_loop(0, pairs // unroll, transport, 0)
        to_left.wait()
        to_right.wait()
        block = 64

        def finish(i, _):
            at = pl.ds(pl.multiple_of(i * block, block), block)
            frm = pl.ds(pl.multiple_of(own + i * block, block), block)
            beside = dot(couple[0, at, :], spot[...]) + dot(couple[1, at, :], spot[...])
            total = jnp.sum(share[at, :], axis=1, keepdims=True)
            coupling = beside - total * spot[frm, :].astype(F32)
            value = (current[at, :] + added[at, :] + coupling) * keep[at, :]
            if sweep == SWEEPS - 1:
                to = pl.ds(pl.multiple_of(edge + i * block, block), block)
                final[0, to, :] = value[:, :LANES]
                final[1, to, 0 : nodes - LANES] = value[:, LANES:]
            else:
                current[at, :] = value
            return 0

        lax.fori_loop(0, rows // block, finish, 0)

    last = [
        ToRight(6, final.at[:, pl.ds(rows, edge)], final.at[:, pl.ds(0, edge)]),
        ToLeft(7, final.at[:, pl.ds(edge, edge)], final.at[:, pl.ds(edge + rows, edge)]),
    ]
    tiles(SWEEPS + 1)
    for copy in meta:
        copy.wait()

    def tally(hits):
        return jnp.sum(hits.astype(F32), axis=1, keepdims=True)

    from_left = tally(owners[1] == me)
    from_right = tally(owners[2] == me)
    stay = tally(owners[0] == me)
    gone = tally(owners[0] == me - 1)
    filled = stay + from_left + from_right
    leading = gone - from_left + MOVE
    line = iota(info.shape, 0)
    info[...] = jnp.where(line == 0, leading, filled)
    for copy in last + bulk:
        copy.wait()


def place_kernel(mass, jac, final, info, out_mass, out_jac, out_final, zeros, sem):
    leading = jnp.max(info[0:1, :]).astype(jnp.int32)
    filled = jnp.max(info[1:2, :]).astype(jnp.int32)
    slots = out_mass.shape[0]
    always = slots // 3
    group = zeros.shape[0]
    for src, dst in ((mass, out_mass), (jac, out_jac)):
        pltpu.make_async_copy(
            src.at[pl.ds(leading, always)], dst.at[pl.ds(0, always)], sem
        ).start()
    zeros[...] = jnp.zeros(zeros.shape, zeros.dtype)
    for src, dst in ((mass, out_mass), (jac, out_jac)):
        for start in range(always, slots, group):
            to = dst.at[pl.ds(start, group)]

            @pl.when(filled >= start + group)
            def _():
                pltpu.make_async_copy(src.at[pl.ds(leading + start, group)], to, sem).start()

            @pl.when(filled <= start)
            def _():
                pltpu.make_async_copy(zeros, to, sem).start()

            @pl.when((filled > start) & (filled < start + group))
            def _():
                def live(i, _):
                    pltpu.make_async_copy(src.at[leading + i], dst.at[i], sem).start()
                    return 0

                def dead(i, _):
                    pltpu.make_async_copy(zeros.at[0], dst.at[i], sem).start()
                    return 0

                lax.fori_loop(start, filled, live, 0)
                lax.fori_loop(filled, start + group, dead, 0)

    variables = out_final.shape[0]
    nodes = out_final.shape[2]
    alive = iota((slots, LANES), 0) < filled
    for var in range(variables):
        at = pl.ds(leading * SLOT + var, slots, stride=SLOT)
        out_final[var, :, 0:LANES] = jnp.where(alive, final[0, at, :], 0.0)
        out_final[var, :, LANES:nodes] = jnp.where(alive, final[1, at, :], 0.0)[:, : nodes - LANES]
    for dst in (out_mass, out_jac):
        pltpu.make_async_copy(dst, dst, sem).wait()


def shards(
    elem_state,
    mass_inverse,
    jacobian,
    elem_order,
    new_owner,
    neighbors,
    penalty,
    closure_in,
    closure_out,
):
    elems, variables, nodes = elem_state.shape
    hid = closure_in.shape[0]
    faces = neighbors.shape[1]
    count = lax.axis_size("dom")
    slots = elems + 2 * MOVE
    rows = elems * SLOT
    span = rows + 2 * REACH * SLOT
    operands = (
        jnp.transpose(elem_state, (1, 0, 2)),
        mass_inverse,
        jacobian,
        elem_order.reshape(1, elems),
        new_owner.reshape(1, elems),
        neighbors.T,
        penalty.T,
        closure_in.T,
        closure_out,
    )
    anywhere = pl.BlockSpec(memory_space=pltpu.HBM)
    near_by = pl.BlockSpec(memory_space=pltpu.VMEM)
    dma = pltpu.SemaphoreType.DMA
    mass, jac, final, info = pl.pallas_call(
        functools.partial(sweep_kernel, count),
        out_shape=(
            pltpu.VMEM((slots, nodes, nodes), BF16),
            pltpu.VMEM((slots, nodes, nodes), BF16),
            pltpu.VMEM((2, (slots + 2 * MOVE) * SLOT, LANES), F32),
            pltpu.VMEM((8, 128), F32),
        ),
        in_specs=[anywhere] * 9,
        out_specs=(near_by,) * 4,
        scratch_shapes=[
            pltpu.VMEM((variables, elems, nodes), BF16),
            pltpu.VMEM((1, elems), jnp.int32),
            pltpu.VMEM((3, 1, elems), jnp.int32),
            pltpu.VMEM((faces, elems), jnp.int32),
            pltpu.VMEM((faces, elems), BF16),
            pltpu.VMEM((variables, hid), BF16),
            pltpu.VMEM((variables, hid), BF16),
            pltpu.VMEM((rows, nodes), F32),
            pltpu.VMEM((rows, nodes), BF16),
            pltpu.VMEM((SWEEPS, span, nodes), BF16),
            pltpu.VMEM((rows, nodes), F32),
            pltpu.VMEM((rows, nodes), F32),
            pltpu.VMEM((2, rows, span), BF16),
            pltpu.VMEM((rows, faces), F32),
            pltpu.VMEM((rows, faces), F32),
            pltpu.VMEM((4 * hid, 4 * SLOT), BF16),
            pltpu.VMEM((4 * SLOT, 4 * hid), BF16),
            dma((7,)),
            dma((3,)),
            dma((SENDS,)),
            dma((SENDS,)),
        ],
        compiler_params=pltpu.CompilerParams(
            collective_id=0, has_side_effects=True, vmem_limit_bytes=24 * 2**20
        ),
        name="sweeps",
    )(*(pltpu.with_memory_space_constraint(operand, pltpu.HBM) for operand in operands))
    out_mass, out_jac, out_final = pl.pallas_call(
        place_kernel,
        out_shape=(
            jax.ShapeDtypeStruct((slots, nodes, nodes), BF16),
            jax.ShapeDtypeStruct((slots, nodes, nodes), BF16),
            jax.ShapeDtypeStruct((variables, slots, nodes), F32),
        ),
        in_specs=[near_by] * 4,
        out_specs=(anywhere, anywhere, near_by),
        scratch_shapes=[pltpu.VMEM((8, nodes, nodes), BF16), dma],
        compiler_params=pltpu.CompilerParams(vmem_limit_bytes=24 * 2**20),
        name="place",
    )(mass, jac, final, info)
    return (jnp.transpose(out_final, (1, 0, 2)), out_mass, out_jac)


def solution(mesh):
    placed = (
        P("dom", None, None),
        P("dom", None, None),
        P("dom", None, None),
        P("dom"),
        P("dom"),
        P("dom", None),
        P("dom", None),
        P(),
        P(),
    )
    return jax.shard_map(
        shards,
        mesh=mesh,
        in_specs=placed,
        out_specs=(P("dom", None, None), P("dom", None, None), P("dom", None, None)),
        check_vma=False,
    )
```

```python
import functools

import jax
import jax.numpy as jnp
from jax import lax
from jax.experimental import pallas as pl
from jax.experimental.pallas import tpu as pltpu
from jax.sharding import PartitionSpec as P

SWEEPS = 2
SLOT = 8
MOVE = 8
REACH = 16
LANES = 128
SCHEDULE = (
    ((0, 0, 5),),
    ((2, 0, 11),),
    ((0, 5, 3), (1, 0, 8)),
    (),
)


def overlap(first, size, other, length):
    low, high = max(first, other), min(first + size, other + length)
    return (low, high) if low < high else None


SENDS = 8 + 2 * sum(len(part) for part in SCHEDULE)
CLOSE = 2
NT = (((1,), (1,)), ((), ()))
NN = (((1,), (0,)), ((), ()))
F32 = jnp.float32
BF16 = jnp.bfloat16


def dot(a, b, dims=NN):
    return lax.dot_general(a, b, dims, preferred_element_type=F32)


def iota(shape, dim):
    return lax.broadcasted_iota(jnp.int32, shape, dim)


def sweep_kernel(
    count,
    state_hbm,
    mass_hbm,
    jac_hbm,
    order_hbm,
    owner_hbm,
    near_hbm,
    penalty_hbm,
    inner_hbm,
    outer_hbm,
    mass,
    jac,
    final,
    info,
    state,
    order,
    owners,
    near,
    penalty,
    inner,
    outer,
    current,
    rounded,
    weighted,
    added,
    keep,
    couple,
    target,
    share,
    first_layer,
    second_layer,
    packed,
    arrived,
    load_sem,
    tile_sem,
    send_sem,
    recv_sem,
):
    me = lax.axis_index("dom")
    right = lax.rem(me + 1, count)
    left = lax.rem(me + count - 1, count)
    elems, nodes = mass_hbm.shape[0], mass_hbm.shape[2]
    rows = elems * SLOT
    edge = MOVE * SLOT
    halo = REACH * SLOT
    core = pl.ds(MOVE, elems)

    small = [
        pltpu.make_async_copy(src, dst, load_sem.at[i])
        for i, (src, dst) in enumerate(
            [
                (state_hbm, state),
                (order_hbm, order),
                (owner_hbm, owners.at[0]),
                (near_hbm, near),
                (penalty_hbm, penalty),
                (inner_hbm, inner),
                (outer_hbm, outer),
            ]
        )
    ]
    half = elems // 2
    mass_load = [
        pltpu.make_async_copy(
            mass_hbm.at[pl.ds(i * half, half)],
            mass.at[pl.ds(MOVE + i * half, half)],
            tile_sem.at[i],
        )
        for i in range(2)
    ]
    jac_load = pltpu.make_async_copy(jac_hbm, jac.at[core], tile_sem.at[2])
    for copy in small + mass_load + [jac_load]:
        copy.start()

    has_left = me > 0
    has_right = me < count - 1
    barrier = pltpu.get_barrier_semaphore()

    def greet(device):
        pl.semaphore_signal(
            barrier, inc=1, device_id=(device,), device_id_type=pl.DeviceIdType.MESH
        )

    @pl.when(has_left)
    def _():
        greet(me - 1)

    @pl.when(has_right)
    def _():
        greet(me + 1)

    pl.semaphore_wait(barrier, has_left.astype(jnp.int32) + has_right.astype(jnp.int32))

    def sender(slot, src, dst, device):
        return pltpu.make_async_remote_copy(
            src_ref=src,
            dst_ref=dst,
            send_sem=send_sem.at[slot],
            recv_sem=recv_sem.at[slot],
            device_id=(device,),
            device_id_type=pl.DeviceIdType.MESH,
        )

    class ToRight:
        def __init__(self, slot, src, dst):
            self.copy = sender(slot, src, dst, right)
            pl.when(has_right)(self.copy.start)

        def wait(self):
            pl.when(has_right)(self.copy.wait_send)
            pl.when(has_left)(self.copy.wait_recv)

    class ToLeft:
        def __init__(self, slot, src, dst):
            self.copy = sender(slot, src, dst, left)
            pl.when(has_left)(self.copy.start)

        def wait(self):
            pl.when(has_left)(self.copy.wait_send)
            pl.when(has_right)(self.copy.wait_recv)

    meta = [ToRight(0, owner_hbm, owners.at[1]), ToLeft(1, owner_hbm, owners.at[2])]
    bulk = []

    def tiles(phase):
        for which, start, size in SCHEDULE[phase]:
            slot = 8 + len(bulk)
            if which == 2:
                part = pl.ds(start, size)
                ends = [(packed.at[side, part], arrived.at[side, part]) for side in range(2)]
            else:
                src, dst = ((mass_hbm, mass), (jac_hbm, jac))[which]
                lanes = pl.ds(0, LANES)
                ends = [
                    (
                        src.at[pl.ds(elems - MOVE + start, size), :, lanes],
                        dst.at[pl.ds(start, size), :, lanes],
                    ),
                    (
                        src.at[pl.ds(start, size), :, lanes],
                        dst.at[pl.ds(MOVE + elems + start, size), :, lanes],
                    ),
                ]
            copies = (ToRight(slot, *ends[0]), ToLeft(slot + 1, *ends[1]))
            bulk.append((which, copies[0]))
            bulk.append((which, copies[1]))

    tiles(0)

    @pl.when(jnp.logical_not(has_left))
    def _():
        for sweep in range(SWEEPS):
            weighted[sweep, 0:halo, :] = jnp.zeros((halo, nodes), BF16)
        owners[1] = jnp.full((1, elems), -1, jnp.int32)

    @pl.when(jnp.logical_not(has_right))
    def _():
        for sweep in range(SWEEPS):
            weighted[sweep, halo + rows : 2 * halo + rows, :] = jnp.zeros((halo, nodes), BF16)
        owners[2] = jnp.full((1, elems), -1, jnp.int32)

    small[0].wait()

    row_of = iota((rows, elems), 0) - SLOT * iota((rows, elems), 1)
    current[...] = sum(
        dot((row_of == var).astype(F32).astype(BF16), state[var]) for var in range(state.shape[0])
    )

    group = 4
    hid = inner.shape[1]
    variables = inner.shape[0]
    wide = group * SLOT
    tall = group * hid
    rest = nodes - LANES
    both = 2 * MOVE
    count_packed = packed.shape[1]

    def other_lanes(i, first):
        array = mass if i < MOVE else jac
        return array, first + i % MOVE

    def pack(side, first):
        for j in range(count_packed):
            pieces = []
            for i in range(both):
                shared = overlap(j * LANES, LANES, i * rest, rest)
                if shared:
                    array, at = other_lanes(i, first)
                    low, high = (lane - i * rest + LANES for lane in shared)
                    pieces.append(array[at, :, low:high])
            packed[side, j] = jnp.concatenate(pieces, axis=1)

    def unpack(side, first):
        for i in range(both):
            pieces = []
            for j in range(count_packed):
                shared = overlap(i * rest, rest, j * LANES, LANES)
                if shared:
                    low, high = (lane - j * LANES for lane in shared)
                    pieces.append(arrived[side, j, :, low:high])
            array, at = other_lanes(i, first)
            array[at, :, LANES:nodes] = jnp.concatenate(pieces, axis=1)

    def prepare():
        for copy in small[1:]:
            copy.wait()

        spread = (iota((rows, elems), 0) // SLOT == iota((rows, elems), 1)).astype(F32).astype(BF16)
        base = me * elems - REACH
        local = jnp.where(near[...] < 0, -1, near[...] - base).astype(F32).astype(BF16)
        faces = near.shape[0]
        near_rows = dot(spread, local, NT)
        lane_var = (iota((rows, faces), 0) % SLOT).astype(F32)
        target[...] = near_rows * SLOT + lane_var
        share[...] = dot(spread, penalty[...], NT)
        orders = jnp.broadcast_to(order[...].astype(F32), (SLOT, elems)).astype(BF16)
        limit = dot(spread, orders, NT)[:, 0:1] + 1.0
        limit = limit * limit * limit
        keep[...] = (iota((rows, nodes), 1).astype(F32) < limit).astype(F32)

        span = couple.shape[2]
        step = 32

        def couple_rows(i, _):
            at = pl.ds(pl.multiple_of(i * step, step), step)
            cols = iota((step, span), 1).astype(F32)
            total = jnp.zeros((step, span), F32)
            for face in range(faces):
                hit = cols == target[at, face : face + 1]
                total = total + jnp.where(hit, share[at, face : face + 1], 0.0)
            high = total.astype(BF16)
            couple[0, at, :] = high
            couple[1, at, :] = (total - high.astype(F32)).astype(BF16)
            return 0

        lax.fori_loop(0, rows // step, couple_rows, 0)

        pick = (iota((variables, wide), 1) % SLOT == iota((variables, wide), 0)).astype(F32).astype(BF16)
        repeat = (iota((hid, tall), 1) % hid == iota((hid, tall), 0)).astype(F32).astype(BF16)
        tn = (((0,), (0,)), ((), ()))
        inner_wide = dot(inner[...], pick, tn).astype(BF16)
        inner_tall = dot(repeat, inner_wide, tn)
        same = iota((tall, wide), 0) // hid == iota((tall, wide), 1) // SLOT
        first_layer[...] = jnp.where(same, inner_tall, 0.0).astype(BF16)
        outer_wide = dot(outer[...], repeat).astype(BF16)
        outer_tall = dot(pick, outer_wide, tn)
        same = iota((wide, tall), 0) // SLOT == iota((wide, tall), 1) // hid
        second_layer[...] = jnp.where(same, outer_tall, 0.0).astype(BF16)

    pairs = elems // 2
    unroll = 4
    upper = iota((2 * SLOT, nodes), 0) < SLOT
    own = halo

    for sweep in range(SWEEPS):
        spot = weighted.at[sweep]
        rounded[...] = current[...].astype(BF16)
        if sweep == 0:
            mass_load[0].wait()

        def weigh(i, _):
            for k in range(unroll):
                pair = i * unroll + k
                at = pl.ds(pl.multiple_of(pair * 2 * SLOT, 2 * SLOT), 2 * SLOT)
                values = rounded[at, :]
                one = dot(values, mass[MOVE + 2 * pair], NT)
                two = dot(values, mass[MOVE + 2 * pair + 1], NT)
                to = pl.ds(pl.multiple_of(own + pair * 2 * SLOT, 2 * SLOT), 2 * SLOT)
                spot[to, :] = jnp.where(upper, one, two).astype(BF16)
            return 0

        lax.fori_loop(0, pairs // unroll // 2, weigh, 0)
        to_left = ToLeft(
            2 + 2 * sweep, spot.at[pl.ds(own, halo)], spot.at[pl.ds(own + rows, halo)]
        )
        if sweep == 0:
            mass_load[1].wait()
        lax.fori_loop(pairs // unroll // 2, pairs // unroll, weigh, 0)
        to_right = ToRight(
            3 + 2 * sweep, spot.at[pl.ds(own + rows - halo, halo)], spot.at[pl.ds(0, halo)]
        )

        if sweep == 0:
            jac_load.wait()
            pack(0, elems)
            pack(1, MOVE)
        tiles(sweep + 1)
        if sweep == 0:
            prepare()

        def close(i, _):
            ats = [
                pl.ds(pl.multiple_of((i * CLOSE + k) * wide, wide), wide) for k in range(CLOSE)
            ]
            inputs = [dot(first_layer[...], rounded[at, :]) for at in ats]
            hidden = [jnp.tanh(value).astype(BF16) for value in inputs]
            for at, value in zip(ats, hidden):
                added[at, :] = dot(second_layer[...], value)
            return 0

        lax.fori_loop(0, rows // wide // CLOSE, close, 0)

        def transport(i, _):
            for k in range(unroll):
                pair = i * unroll + k
                at = pl.ds(pl.multiple_of(pair * 2 * SLOT, 2 * SLOT), 2 * SLOT)
                frm = pl.ds(pl.multiple_of(own + pair * 2 * SLOT, 2 * SLOT), 2 * SLOT)
                values = spot[frm, :]
                one = dot(values, jac[MOVE + 2 * pair])
                two = dot(values, jac[MOVE + 2 * pair + 1])
                added[at, :] = added[at, :] + jnp.where(upper, one, two)
            return 0

        lax.fori_loop(0, pairs // unroll, transport, 0)
        to_left.wait()
        to_right.wait()
        block = 64

        def finish(i, _):
            at = pl.ds(pl.multiple_of(i * block, block), block)
            frm = pl.ds(pl.multiple_of(own + i * block, block), block)
            beside = dot(couple[0, at, :], spot[...]) + dot(couple[1, at, :], spot[...])
            total = jnp.sum(share[at, :], axis=1, keepdims=True)
            coupling = beside - total * spot[frm, :].astype(F32)
            value = (current[at, :] + added[at, :] + coupling) * keep[at, :]
            if sweep == SWEEPS - 1:
                to = pl.ds(pl.multiple_of(edge + i * block, block), block)
                final[0, to, :] = value[:, :LANES]
                final[1, to, 0 : nodes - LANES] = value[:, LANES:]
            else:
                current[at, :] = value
            return 0

        lax.fori_loop(0, rows // block, finish, 0)

    last = [
        ToRight(6, final.at[:, pl.ds(rows, edge)], final.at[:, pl.ds(0, edge)]),
        ToLeft(7, final.at[:, pl.ds(edge, edge)], final.at[:, pl.ds(edge + rows, edge)]),
    ]
    tiles(SWEEPS + 1)
    for copy in meta:
        copy.wait()

    def tally(hits):
        return jnp.sum(hits.astype(F32), axis=1, keepdims=True)

    from_left = tally(owners[1] == me)
    from_right = tally(owners[2] == me)
    stay = tally(owners[0] == me)
    gone = tally(owners[0] == me - 1)
    filled = stay + from_left + from_right
    leading = gone - from_left + MOVE
    line = iota(info.shape, 0)
    info[...] = jnp.where(line == 0, leading, filled)
    for which, copy in bulk:
        if which == 2:
            copy.wait()
    unpack(0, 0)
    unpack(1, MOVE + elems)
    for copy in last + [copy for which, copy in bulk if which != 2]:
        copy.wait()


def place_kernel(
    mass, jac, final, info, out_mass, out_jac, out_final, zeros, planes, sem, planes_sem
):
    leading = jnp.max(info[0:1, :]).astype(jnp.int32)
    filled = jnp.max(info[1:2, :]).astype(jnp.int32)
    slots = out_mass.shape[0]
    always = slots // 3
    group = zeros.shape[0]
    for src, dst in ((mass, out_mass), (jac, out_jac)):
        pltpu.make_async_copy(
            src.at[pl.ds(leading, always)], dst.at[pl.ds(0, always)], sem
        ).start()
    zeros[...] = jnp.zeros(zeros.shape, zeros.dtype)
    for src, dst in ((mass, out_mass), (jac, out_jac)):
        for start in range(always, slots, group):
            to = dst.at[pl.ds(start, group)]

            @pl.when(filled >= start + group)
            def _():
                pltpu.make_async_copy(src.at[pl.ds(leading + start, group)], to, sem).start()

            @pl.when(filled <= start)
            def _():
                pltpu.make_async_copy(zeros, to, sem).start()

            @pl.when((filled > start) & (filled < start + group))
            def _():
                def live(i, _):
                    pltpu.make_async_copy(src.at[leading + i], dst.at[i], sem).start()
                    return 0

                def dead(i, _):
                    pltpu.make_async_copy(zeros.at[0], dst.at[i], sem).start()
                    return 0

                lax.fori_loop(start, filled, live, 0)
                lax.fori_loop(filled, start + group, dead, 0)

    variables = out_final.shape[0]
    nodes = out_final.shape[2]
    alive = iota((slots, LANES), 0) < filled
    for var in range(variables):
        at = pl.ds(leading * SLOT + var, slots, stride=SLOT)
        planes[var, :, 0:LANES] = jnp.where(alive, final[0, at, :], 0.0)
        planes[var, :, LANES:nodes] = jnp.where(alive, final[1, at, :], 0.0)[:, : nodes - LANES]
    states = pltpu.make_async_copy(planes, out_final, planes_sem)
    states.start()
    for dst in (out_mass, out_jac):
        pltpu.make_async_copy(dst, dst, sem).wait()
    states.wait()


def shards(
    elem_state,
    mass_inverse,
    jacobian,
    elem_order,
    new_owner,
    neighbors,
    penalty,
    closure_in,
    closure_out,
):
    elems, variables, nodes = elem_state.shape
    hid = closure_in.shape[0]
    faces = neighbors.shape[1]
    count = lax.axis_size("dom")
    slots = elems + 2 * MOVE
    rows = elems * SLOT
    span = rows + 2 * REACH * SLOT
    full = -(-2 * MOVE * (nodes - LANES) // LANES)
    operands = (
        jnp.transpose(elem_state, (1, 0, 2)),
        mass_inverse,
        jacobian,
        elem_order.reshape(1, elems),
        new_owner.reshape(1, elems),
        neighbors.T,
        penalty.T,
        closure_in.T,
        closure_out,
    )
    anywhere = pl.BlockSpec(memory_space=pltpu.HBM)
    near_by = pl.BlockSpec(memory_space=pltpu.VMEM)
    dma = pltpu.SemaphoreType.DMA
    mass, jac, final, info = pl.pallas_call(
        functools.partial(sweep_kernel, count),
        out_shape=(
            pltpu.VMEM((slots, nodes, nodes), BF16),
            pltpu.VMEM((slots, nodes, nodes), BF16),
            pltpu.VMEM((2, (slots + 2 * MOVE) * SLOT, LANES), F32),
            pltpu.VMEM((8, 128), F32),
        ),
        in_specs=[anywhere] * 9,
        out_specs=(near_by,) * 4,
        scratch_shapes=[
            pltpu.VMEM((variables, elems, nodes), BF16),
            pltpu.VMEM((1, elems), jnp.int32),
            pltpu.VMEM((3, 1, elems), jnp.int32),
            pltpu.VMEM((faces, elems), jnp.int32),
            pltpu.VMEM((faces, elems), BF16),
            pltpu.VMEM((variables, hid), BF16),
            pltpu.VMEM((variables, hid), BF16),
            pltpu.VMEM((rows, nodes), F32),
            pltpu.VMEM((rows, nodes), BF16),
            pltpu.VMEM((SWEEPS, span, nodes), BF16),
            pltpu.VMEM((rows, nodes), F32),
            pltpu.VMEM((rows, nodes), F32),
            pltpu.VMEM((2, rows, span), BF16),
            pltpu.VMEM((rows, faces), F32),
            pltpu.VMEM((rows, faces), F32),
            pltpu.VMEM((4 * hid, 4 * SLOT), BF16),
            pltpu.VMEM((4 * SLOT, 4 * hid), BF16),
            pltpu.VMEM((2, full, nodes, LANES), BF16),
            pltpu.VMEM((2, full, nodes, LANES), BF16),
            dma((7,)),
            dma((3,)),
            dma((SENDS,)),
            dma((SENDS,)),
        ],
        compiler_params=pltpu.CompilerParams(
            collective_id=0, has_side_effects=True, vmem_limit_bytes=24 * 2**20
        ),
        name="sweeps",
    )(*(pltpu.with_memory_space_constraint(operand, pltpu.HBM) for operand in operands))
    out_mass, out_jac, out_final = pl.pallas_call(
        place_kernel,
        out_shape=(
            jax.ShapeDtypeStruct((slots, nodes, nodes), BF16),
            jax.ShapeDtypeStruct((slots, nodes, nodes), BF16),
            jax.ShapeDtypeStruct((variables, slots, nodes), F32),
        ),
        in_specs=[near_by] * 4,
        out_specs=(anywhere,) * 3,
        scratch_shapes=[
            pltpu.VMEM((8, nodes, nodes), BF16),
            pltpu.VMEM((variables, slots, nodes), F32),
            dma,
            dma,
        ],
        compiler_params=pltpu.CompilerParams(vmem_limit_bytes=24 * 2**20),
        name="place",
    )(mass, jac, final, info)
    return (jnp.transpose(out_final, (1, 0, 2)), out_mass, out_jac)


def solution(mesh):
    placed = (
        P("dom", None, None),
        P("dom", None, None),
        P("dom", None, None),
        P("dom"),
        P("dom"),
        P("dom", None),
        P("dom", None),
        P(),
        P(),
    )
    return jax.shard_map(
        shards,
        mesh=mesh,
        in_specs=placed,
        out_specs=(P("dom", None, None), P("dom", None, None), P("dom", None, None)),
        check_vma=False,
    )
```

```python
import functools

import jax
import jax.numpy as jnp
from jax import lax
from jax.experimental import pallas as pl
from jax.experimental.pallas import tpu as pltpu
from jax.sharding import PartitionSpec as P

SWEEPS = 2
SLOT = 8
MOVE = 8
REACH = 16
LANES = 128
SCHEDULE = (
    ((0, 0, 5),),
    ((2, 0, 11),),
    ((0, 5, 3), (1, 0, 8)),
    (),
)


def overlap(first, size, other, length):
    low, high = max(first, other), min(first + size, other + length)
    return (low, high) if low < high else None


SENDS = 8 + 2 * sum(len(part) for part in SCHEDULE)
CLOSE = 2
NT = (((1,), (1,)), ((), ()))
NN = (((1,), (0,)), ((), ()))
F32 = jnp.float32
BF16 = jnp.bfloat16


def dot(a, b, dims=NN):
    return lax.dot_general(a, b, dims, preferred_element_type=F32)


def iota(shape, dim):
    return lax.broadcasted_iota(jnp.int32, shape, dim)


def sweep_kernel(
    count,
    state_hbm,
    mass_hbm,
    jac_hbm,
    order_hbm,
    owner_hbm,
    near_hbm,
    penalty_hbm,
    inner_hbm,
    outer_hbm,
    mass,
    jac,
    final,
    info,
    state,
    order,
    owners,
    near,
    penalty,
    inner,
    outer,
    current,
    rounded,
    weighted,
    added,
    keep,
    couple,
    target,
    share,
    first_layer,
    second_layer,
    packed,
    arrived,
    edges,
    load_sem,
    tile_sem,
    send_sem,
    recv_sem,
):
    me = lax.axis_index("dom")
    right = lax.rem(me + 1, count)
    left = lax.rem(me + count - 1, count)
    elems, nodes = mass_hbm.shape[0], mass_hbm.shape[2]
    rows = elems * SLOT
    variables = state.shape[0]
    halo = REACH * variables
    core = pl.ds(MOVE, elems)

    has_left = me > 0
    has_right = me < count - 1
    barrier = pltpu.get_barrier_semaphore()

    def greet(device):
        pl.semaphore_signal(
            barrier, inc=1, device_id=(device,), device_id_type=pl.DeviceIdType.MESH
        )

    @pl.when(has_left)
    def _():
        greet(me - 1)

    @pl.when(has_right)
    def _():
        greet(me + 1)

    small = [
        pltpu.make_async_copy(src, dst, load_sem.at[i])
        for i, (src, dst) in enumerate(
            [
                (state_hbm, state),
                (order_hbm, order),
                (owner_hbm, owners.at[0]),
                (near_hbm, near),
                (penalty_hbm, penalty),
                (inner_hbm, inner),
                (outer_hbm, outer),
            ]
        )
    ]
    half = elems // 2
    mass_load = [
        pltpu.make_async_copy(
            mass_hbm.at[pl.ds(i * half, half)],
            mass.at[pl.ds(MOVE + i * half, half)],
            tile_sem.at[i],
        )
        for i in range(2)
    ]
    jac_load = pltpu.make_async_copy(jac_hbm, jac.at[core], tile_sem.at[2])
    for copy in small + mass_load + [jac_load]:
        copy.start()

    pl.semaphore_wait(barrier, has_left.astype(jnp.int32) + has_right.astype(jnp.int32))

    def sender(slot, src, dst, device):
        return pltpu.make_async_remote_copy(
            src_ref=src,
            dst_ref=dst,
            send_sem=send_sem.at[slot],
            recv_sem=recv_sem.at[slot],
            device_id=(device,),
            device_id_type=pl.DeviceIdType.MESH,
        )

    class ToRight:
        def __init__(self, slot, src, dst):
            self.copy = sender(slot, src, dst, right)
            pl.when(has_right)(self.copy.start)

        def wait(self):
            pl.when(has_right)(self.copy.wait_send)
            pl.when(has_left)(self.copy.wait_recv)

    class ToLeft:
        def __init__(self, slot, src, dst):
            self.copy = sender(slot, src, dst, left)
            pl.when(has_left)(self.copy.start)

        def wait(self):
            pl.when(has_left)(self.copy.wait_send)
            pl.when(has_right)(self.copy.wait_recv)

    bulk = []

    def tiles(phase):
        for which, start, size in SCHEDULE[phase]:
            slot = 8 + len(bulk)
            if which == 2:
                part = pl.ds(start, size)
                ends = [(packed.at[side, part], arrived.at[side, part]) for side in range(2)]
            else:
                src, dst = ((mass_hbm, mass), (jac_hbm, jac))[which]
                lanes = pl.ds(0, LANES)
                ends = [
                    (
                        src.at[pl.ds(elems - MOVE + start, size), :, lanes],
                        dst.at[pl.ds(start, size), :, lanes],
                    ),
                    (
                        src.at[pl.ds(start, size), :, lanes],
                        dst.at[pl.ds(MOVE + elems + start, size), :, lanes],
                    ),
                ]
            copies = (ToRight(slot, *ends[0]), ToLeft(slot + 1, *ends[1]))
            bulk.append((which, copies[0]))
            bulk.append((which, copies[1]))

    tiles(0)
    meta = [ToRight(0, owner_hbm, owners.at[1]), ToLeft(1, owner_hbm, owners.at[2])]

    @pl.when(jnp.logical_not(has_left))
    def _():
        for sweep in range(SWEEPS):
            weighted[sweep, 0:halo, :] = jnp.zeros((halo, nodes), BF16)
        owners[1] = jnp.full((1, elems), -1, jnp.int32)

    @pl.when(jnp.logical_not(has_right))
    def _():
        for sweep in range(SWEEPS):
            weighted[sweep, halo + rows : 2 * halo + rows, :] = jnp.zeros((halo, nodes), BF16)
        owners[2] = jnp.full((1, elems), -1, jnp.int32)

    small[0].wait()

    row_of = iota((rows, elems), 0) - SLOT * iota((rows, elems), 1)
    current[...] = sum(
        dot((row_of == var).astype(F32).astype(BF16), state[var]) for var in range(state.shape[0])
    )

    group = 4
    hid = inner.shape[1]
    wide = group * SLOT
    tall = group * hid
    rest = nodes - LANES
    both = 2 * MOVE
    count_packed = packed.shape[1]

    def other_lanes(i, first):
        array = mass if i < MOVE else jac
        return array, first + i % MOVE

    def pack(side, first):
        for j in range(count_packed):
            pieces = []
            for i in range(both):
                shared = overlap(j * LANES, LANES, i * rest, rest)
                if shared:
                    array, at = other_lanes(i, first)
                    low, high = (lane - i * rest + LANES for lane in shared)
                    pieces.append(array[at, :, low:high])
            packed[side, j] = jnp.concatenate(pieces, axis=1)

    def unpack(side, first):
        for i in range(both):
            pieces = []
            for j in range(count_packed):
                shared = overlap(i * rest, rest, j * LANES, LANES)
                if shared:
                    low, high = (lane - j * LANES for lane in shared)
                    pieces.append(arrived[side, j, :, low:high])
            array, at = other_lanes(i, first)
            array[at, :, LANES:nodes] = jnp.concatenate(pieces, axis=1)

    def prepare():
        for copy in small[1:]:
            copy.wait()

        spread = (iota((rows, elems), 0) // SLOT == iota((rows, elems), 1)).astype(F32).astype(BF16)
        base = me * elems - REACH
        local = jnp.where(near[...] < 0, -1, near[...] - base).astype(F32).astype(BF16)
        faces = near.shape[0]
        near_rows = dot(spread, local, NT)
        lane_var = (iota((rows, faces), 0) % SLOT).astype(F32)
        before = lane_var * REACH + near_rows
        inside = (near_rows - REACH) * SLOT + lane_var + halo
        after = before + (halo + rows - REACH - elems)
        column = jnp.where(
            near_rows < REACH, before, jnp.where(near_rows < REACH + elems, inside, after)
        )
        target[...] = jnp.where((near_rows < 0) | (lane_var >= variables), -1.0, column)
        share[...] = dot(spread, penalty[...], NT)
        orders = jnp.broadcast_to(order[...].astype(F32), (SLOT, elems)).astype(BF16)
        limit = dot(spread, orders, NT)[:, 0:1] + 1.0
        limit = limit * limit * limit
        keep[...] = (iota((rows, nodes), 1).astype(F32) < limit).astype(F32)

        span = couple.shape[2]
        step = 32

        def couple_rows(i, _):
            at = pl.ds(pl.multiple_of(i * step, step), step)
            cols = iota((step, span), 1).astype(F32)
            total = jnp.zeros((step, span), F32)
            for face in range(faces):
                hit = cols == target[at, face : face + 1]
                total = total + jnp.where(hit, share[at, face : face + 1], 0.0)
            high = total.astype(BF16)
            couple[0, at, :] = high
            couple[1, at, :] = (total - high.astype(F32)).astype(BF16)
            return 0

        lax.fori_loop(0, rows // step, couple_rows, 0)

        pick = (iota((variables, wide), 1) % SLOT == iota((variables, wide), 0)).astype(F32).astype(BF16)
        repeat = (iota((hid, tall), 1) % hid == iota((hid, tall), 0)).astype(F32).astype(BF16)
        tn = (((0,), (0,)), ((), ()))
        inner_wide = dot(inner[...], pick, tn).astype(BF16)
        inner_tall = dot(repeat, inner_wide, tn)
        same = iota((tall, wide), 0) // hid == iota((tall, wide), 1) // SLOT
        first_layer[...] = jnp.where(same, inner_tall, 0.0).astype(BF16)
        outer_wide = dot(outer[...], repeat).astype(BF16)
        outer_tall = dot(pick, outer_wide, tn)
        same = iota((wide, tall), 0) // SLOT == iota((wide, tall), 1) // hid
        second_layer[...] = jnp.where(same, outer_tall, 0.0).astype(BF16)

    pairs = elems // 2
    unroll = 4
    upper = iota((2 * SLOT, nodes), 0) < SLOT
    own = halo
    reach = REACH * SLOT
    goal = iota((halo, reach), 0)
    taken = (goal % REACH) * SLOT + goal // REACH
    slim = (taken == iota((halo, reach), 1)).astype(F32).astype(BF16)

    for sweep in range(SWEEPS):
        spot = weighted.at[sweep]
        rounded[...] = current[...].astype(BF16)
        if sweep == 0:
            mass_load[0].wait()

        def weigh(i, _):
            for k in range(unroll):
                pair = i * unroll + k
                at = pl.ds(pl.multiple_of(pair * 2 * SLOT, 2 * SLOT), 2 * SLOT)
                values = rounded[at, :]
                one = dot(values, mass[MOVE + 2 * pair], NT)
                two = dot(values, mass[MOVE + 2 * pair + 1], NT)
                to = pl.ds(pl.multiple_of(own + pair * 2 * SLOT, 2 * SLOT), 2 * SLOT)
                spot[to, :] = jnp.where(upper, one, two).astype(BF16)
            return 0

        lax.fori_loop(0, pairs // unroll // 2, weigh, 0)
        edges[2 * sweep] = dot(slim, spot[own : own + reach, :]).astype(BF16)
        to_left = ToLeft(2 + 2 * sweep, edges.at[2 * sweep], spot.at[pl.ds(own + rows, halo)])
        if sweep == 0:
            mass_load[1].wait()
        lax.fori_loop(pairs // unroll // 2, pairs // unroll, weigh, 0)
        edges[2 * sweep + 1] = dot(slim, spot[own + rows - reach : own + rows, :]).astype(BF16)
        to_right = ToRight(3 + 2 * sweep, edges.at[2 * sweep + 1], spot.at[pl.ds(0, halo)])
        if sweep == 0:
            jac_load.wait()
            pack(0, elems)
            pack(1, MOVE)
        tiles(sweep + 1)
        if sweep == 0:
            prepare()

        def close(i, _):
            ats = [
                pl.ds(pl.multiple_of((i * CLOSE + k) * wide, wide), wide) for k in range(CLOSE)
            ]
            inputs = [dot(first_layer[...], rounded[at, :]) for at in ats]
            hidden = [jnp.tanh(value).astype(BF16) for value in inputs]
            for at, value in zip(ats, hidden):
                added[at, :] = dot(second_layer[...], value)
            return 0

        lax.fori_loop(0, rows // wide // CLOSE, close, 0)

        def transport(i, _):
            for k in range(unroll):
                pair = i * unroll + k
                at = pl.ds(pl.multiple_of(pair * 2 * SLOT, 2 * SLOT), 2 * SLOT)
                frm = pl.ds(pl.multiple_of(own + pair * 2 * SLOT, 2 * SLOT), 2 * SLOT)
                values = spot[frm, :]
                one = dot(values, jac[MOVE + 2 * pair])
                two = dot(values, jac[MOVE + 2 * pair + 1])
                added[at, :] = added[at, :] + jnp.where(upper, one, two)
            return 0

        lax.fori_loop(0, pairs // unroll, transport, 0)
        to_left.wait()
        to_right.wait()
        block = 64

        def finish(i, _):
            at = pl.ds(pl.multiple_of(i * block, block), block)
            frm = pl.ds(pl.multiple_of(own + i * block, 2 * SLOT), block)
            beside = dot(couple[0, at, :], spot[...]) + dot(couple[1, at, :], spot[...])
            total = jnp.sum(share[at, :], axis=1, keepdims=True)
            coupling = beside - total * spot[frm, :].astype(F32)
            value = (current[at, :] + added[at, :] + coupling) * keep[at, :]
            if sweep == SWEEPS - 1:
                many = block // SLOT
                to = pl.ds(MOVE + i * many, many)
                cut = value.reshape(many, SLOT, nodes)
                final[0, to] = cut[:, :, :LANES]
                final[1, to, :, 0 : nodes - LANES] = cut[:, :, LANES:]
            else:
                current[at, :] = value
            return 0

        lax.fori_loop(0, rows // block, finish, 0)

    used = pl.ds(0, variables)
    beyond = pl.ds(MOVE + elems, MOVE)
    last = [
        ToRight(6, final.at[:, pl.ds(elems, MOVE), used], final.at[:, pl.ds(0, MOVE), used]),
        ToLeft(7, final.at[:, pl.ds(MOVE, MOVE), used], final.at[:, beyond, used]),
    ]
    tiles(SWEEPS + 1)
    for copy in meta:
        copy.wait()

    def tally(hits):
        return jnp.sum(hits.astype(F32), axis=1, keepdims=True)

    from_left = tally(owners[1] == me)
    from_right = tally(owners[2] == me)
    stay = tally(owners[0] == me)
    gone = tally(owners[0] == me - 1)
    filled = stay + from_left + from_right
    leading = gone - from_left + MOVE
    line = iota(info.shape, 0)
    info[...] = jnp.where(line == 0, leading, filled)
    for which, copy in bulk:
        if which == 2:
            copy.wait()
    unpack(0, 0)
    unpack(1, MOVE + elems)
    for copy in last + [copy for which, copy in bulk if which != 2]:
        copy.wait()


def place_kernel(
    mass, jac, final, info, out_mass, out_jac, out_final, zeros, planes, sem, planes_sem
):
    leading = jnp.max(info[0:1, :]).astype(jnp.int32)
    filled = jnp.max(info[1:2, :]).astype(jnp.int32)
    slots = out_mass.shape[0]
    always = slots // 3
    group = zeros.shape[0]
    for src, dst in ((mass, out_mass), (jac, out_jac)):
        pltpu.make_async_copy(
            src.at[pl.ds(leading, always)], dst.at[pl.ds(0, always)], sem
        ).start()
    zeros[...] = jnp.zeros(zeros.shape, zeros.dtype)
    for src, dst in ((mass, out_mass), (jac, out_jac)):
        for start in range(always, slots, group):
            to = dst.at[pl.ds(start, group)]

            @pl.when(filled >= start + group)
            def _():
                pltpu.make_async_copy(src.at[pl.ds(leading + start, group)], to, sem).start()

            @pl.when(filled <= start)
            def _():
                pltpu.make_async_copy(zeros, to, sem).start()

            @pl.when((filled > start) & (filled < start + group))
            def _():
                def live(i, _):
                    pltpu.make_async_copy(src.at[leading + i], dst.at[i], sem).start()
                    return 0

                def dead(i, _):
                    pltpu.make_async_copy(zeros.at[0], dst.at[i], sem).start()
                    return 0

                lax.fori_loop(start, filled, live, 0)
                lax.fori_loop(filled, start + group, dead, 0)

    variables = out_final.shape[0]
    nodes = out_final.shape[2]
    alive = iota((slots, LANES), 0) < filled
    for var in range(variables):
        at = pl.ds(leading, slots)
        planes[var, :, 0:LANES] = jnp.where(alive, final[0, at, var, :], 0.0)
        planes[var, :, LANES:nodes] = jnp.where(alive, final[1, at, var, :], 0.0)[:, : nodes - LANES]
    states = pltpu.make_async_copy(planes, out_final, planes_sem)
    states.start()
    for dst in (out_mass, out_jac):
        pltpu.make_async_copy(dst, dst, sem).wait()
    states.wait()


def shards(
    elem_state,
    mass_inverse,
    jacobian,
    elem_order,
    new_owner,
    neighbors,
    penalty,
    closure_in,
    closure_out,
):
    elems, variables, nodes = elem_state.shape
    hid = closure_in.shape[0]
    faces = neighbors.shape[1]
    count = lax.axis_size("dom")
    slots = elems + 2 * MOVE
    rows = elems * SLOT
    span = rows + 2 * REACH * variables
    full = -(-2 * MOVE * (nodes - LANES) // LANES)
    operands = (
        jnp.transpose(elem_state, (1, 0, 2)),
        mass_inverse,
        jacobian,
        elem_order.reshape(1, elems),
        new_owner.reshape(1, elems),
        neighbors.T,
        penalty.T,
        closure_in.T,
        closure_out,
    )
    anywhere = pl.BlockSpec(memory_space=pltpu.HBM)
    near_by = pl.BlockSpec(memory_space=pltpu.VMEM)
    dma = pltpu.SemaphoreType.DMA
    mass, jac, final, info = pl.pallas_call(
        functools.partial(sweep_kernel, count),
        out_shape=(
            pltpu.VMEM((slots, nodes, nodes), BF16),
            pltpu.VMEM((slots, nodes, nodes), BF16),
            pltpu.VMEM((2, slots + 2 * MOVE, SLOT, LANES), F32),
            pltpu.VMEM((8, 128), F32),
        ),
        in_specs=[anywhere] * 9,
        out_specs=(near_by,) * 4,
        scratch_shapes=[
            pltpu.VMEM((variables, elems, nodes), BF16),
            pltpu.VMEM((1, elems), jnp.int32),
            pltpu.VMEM((3, 1, elems), jnp.int32),
            pltpu.VMEM((faces, elems), jnp.int32),
            pltpu.VMEM((faces, elems), BF16),
            pltpu.VMEM((variables, hid), BF16),
            pltpu.VMEM((variables, hid), BF16),
            pltpu.VMEM((rows, nodes), F32),
            pltpu.VMEM((rows, nodes), BF16),
            pltpu.VMEM((SWEEPS, span, nodes), BF16),
            pltpu.VMEM((rows, nodes), F32),
            pltpu.VMEM((rows, nodes), F32),
            pltpu.VMEM((2, rows, span), BF16),
            pltpu.VMEM((rows, faces), F32),
            pltpu.VMEM((rows, faces), F32),
            pltpu.VMEM((4 * hid, 4 * SLOT), BF16),
            pltpu.VMEM((4 * SLOT, 4 * hid), BF16),
            pltpu.VMEM((2, full, nodes, LANES), BF16),
            pltpu.VMEM((2, full, nodes, LANES), BF16),
            pltpu.VMEM((2 * SWEEPS, REACH * variables, nodes), BF16),
            dma((7,)),
            dma((3,)),
            dma((SENDS,)),
            dma((SENDS,)),
        ],
        compiler_params=pltpu.CompilerParams(
            collective_id=0, has_side_effects=True, vmem_limit_bytes=24 * 2**20
        ),
        name="sweeps",
    )(*(pltpu.with_memory_space_constraint(operand, pltpu.HBM) for operand in operands))
    out_mass, out_jac, out_final = pl.pallas_call(
        place_kernel,
        out_shape=(
            jax.ShapeDtypeStruct((slots, nodes, nodes), BF16),
            jax.ShapeDtypeStruct((slots, nodes, nodes), BF16),
            jax.ShapeDtypeStruct((variables, slots, nodes), F32),
        ),
        in_specs=[near_by] * 4,
        out_specs=(anywhere,) * 3,
        scratch_shapes=[
            pltpu.VMEM((8, nodes, nodes), BF16),
            pltpu.VMEM((variables, slots, nodes), F32),
            dma,
            dma,
        ],
        compiler_params=pltpu.CompilerParams(vmem_limit_bytes=24 * 2**20),
        name="place",
    )(mass, jac, final, info)
    return (jnp.transpose(out_final, (1, 0, 2)), out_mass, out_jac)


def solution(mesh):
    placed = (
        P("dom", None, None),
        P("dom", None, None),
        P("dom", None, None),
        P("dom"),
        P("dom"),
        P("dom", None),
        P("dom", None),
        P(),
        P(),
    )
    return jax.shard_map(
        shards,
        mesh=mesh,
        in_specs=placed,
        out_specs=(P("dom", None, None), P("dom", None, None), P("dom", None, None)),
        check_vma=False,
    )
```
